32 devices in a mesh: pour: 2 (over x), brick: 16 (over z, y, core).
Axes of the slice: x: 2, y: 2, z: 4, core: 2. Of those that a mesh axis runs over, the one named last changes fastest.
Arguments:
- initial_voxel_degrees: float32 [256, 256, 256], P(('pour', 'brick')), parts along dimension 0, may hold values from -2 to 4
- alloy_tag_per_voxel: int32 [128, 256, 256], P('brick'), may hold values from 0 to 7
- thermal_conductance_per_alloy: float32 [8], replicated, may hold values from 0.2 to 1
- specific_storage_per_alloy: float32 [8], replicated, may hold values from 1 to 4
- bore_boundary_positions: int32 [16, 32, 256], P('brick'), may hold values from 0 to 524287
- surface_transfer_coefficient: float32 [16, 32], P('brick'), may hold values from 0 to 18
- surface_over_flow_ratio: float32 [32], replicated, may hold values from 0 to 1
- flow_direction_flag: int32 [32], replicated, may hold values from 0 to 1
- entry_coolant_degrees: float32 [64], P('pour'), parts along dimension 0, may hold values from -1 to 0
Outputs:
- die_temperature: float32 [256, 256, 256], P(('pour', 'brick')), parts along dimension 0
- coolant_mid: float32 [32, 32], P(('pour', 'brick')), parts along dimension 0
The draws below stay inside these ranges and needn't reach their ends.
There are 2 independent parts, one for each index of `pour`. The reference program is written for one: setup_inputs(seed, part) draws one part's arguments, and reference() takes and returns one part's arrays. A program takes and returns all parts, laid end to end along the dimension named above; an argument that names none is the same for every part. Nothing has to cross between parts.
Inputs may be any that keep to these rules, and one draw needn't show every extreme that they name: `bore_boundary_positions`: indices refer to cells of the segment's own brick.
All inputs are finite; a program needn't handle non-finite values.
Results may differ from the reference program's by a relative error of at most 0.00006.
Values sent between devices are 32-bit elements; how exact they have to be, the bound alone decides.
A program may use at most 64 MiB of HBM per device.

```python
import math
import jax
import jax.numpy as jnp
from jax import lax

CX = 8
NY = 256
NZ = 256
STEPS = 3
LINES = 32
WALL = 256
MATS = 8
NXT = 128
N_BRICK = 16


def draw_initial_voxel_degrees(key, part):
    array_extent = (CX * N_BRICK, NY, NZ)
    first = jax.random.fold_in(key, 0)
    rough = jnp.clip(jax.random.normal(first, array_extent, jnp.float32), -4.0, 4.0)
    return 1.0 + 0.6 * rough


def draw_surface_transfer_coefficient(key, part):
    array_extent = (N_BRICK, LINES)
    first, second_operand, third = jax.random.split(key, 3)
    baseline_value = jnp.exp(jax.random.uniform(first, array_extent, jnp.float32, jnp.log(0.5), jnp.log(2.0)))
    pulse_count = jax.random.uniform(second_operand, array_extent, jnp.float32) < 2.0 / N_BRICK
    total_quantity = jax.random.uniform(third, array_extent, jnp.float32, 0.2, 0.5) * N_BRICK
    return baseline_value + jnp.where(pulse_count, total_quantity, 0.0)


def draw_surface_over_flow_ratio(key, part):
    return jnp.exp(jax.random.uniform(key, (LINES,), jnp.float32, jnp.log(0.25), jnp.log(8.0))) / N_BRICK


def touch_ends(entries, rng, low, largest):
    shape = entries.shape
    index_at = [jax.random.randint(jax.random.fold_in(rng, axis), (), 0, shape[axis]) for axis in range(len(shape))]
    entries = entries.at[tuple(index_at)].set(low)
    longest = shape.index(max(shape))
    index_at[longest] = (index_at[longest] + 1) % shape[longest]
    return entries.at[tuple(index_at)].set(largest)


def setup_inputs(seed: int = 0, part: int = 0) -> dict:
    splits = jax.random.split(jax.random.key(seed), 10)
    own_keys = jax.random.split(jax.random.fold_in(splits[9], part), 10)
    return {
        "initial_voxel_degrees": draw_initial_voxel_degrees(jax.random.fold_in(jax.random.fold_in(splits[9], part), 71), part),
        "alloy_tag_per_voxel": touch_ends(jax.random.randint(splits[1], (NXT, NY, NZ), 0, MATS), jax.random.fold_in(splits[1], 1), 0, MATS - 1).astype(jnp.int32),
        "thermal_conductance_per_alloy": jnp.clip(jnp.exp(jax.random.uniform(splits[2], (MATS,), jnp.float32, math.log(0.2), math.log(1.0))), 0.2, 1.0),
        "specific_storage_per_alloy": jnp.clip(jnp.exp(jax.random.uniform(splits[3], (MATS,), jnp.float32, math.log(1.0), math.log(4.0))), 1.0, 4.0),
        "bore_boundary_positions": touch_ends(jax.random.randint(splits[4], (N_BRICK, LINES, WALL), 0, CX * NY * NZ), jax.random.fold_in(splits[4], 1), 0, (CX * NY * NZ) - 1).astype(jnp.int32),
        "surface_transfer_coefficient": draw_surface_transfer_coefficient(jax.random.fold_in(splits[9], 71), part),
        "surface_over_flow_ratio": draw_surface_over_flow_ratio(jax.random.fold_in(splits[9], 71), part),
        "flow_direction_flag": touch_ends(jax.random.randint(splits[7], (LINES,), 0, 2), jax.random.fold_in(splits[7], 1), 0, 1).astype(jnp.int32),
        "entry_coolant_degrees": jnp.clip(jax.random.uniform(own_keys[8], (LINES,), jnp.float32, -1.0, 0.0), -1.0, 0.0),
    }


def lookup(alloy_tag_per_voxel, table):
    result = jnp.zeros(alloy_tag_per_voxel.shape, table.dtype)
    for material in range(table.shape[0]):
        result = jnp.where(alloy_tag_per_voxel == material, table[material], result)
    return result


def face_mean(left, right):
    return 2.0 * left * right / (left + right + 1e-30)


def advance(updated_thermal_state, conduct, coeffs):
    center = updated_thermal_state[1:-1]
    center_cond = conduct[1:-1]
    fluxes = face_mean(center_cond, conduct[2:]) * (updated_thermal_state[2:] - center)
    fluxes = fluxes + face_mean(center_cond, conduct[:-2]) * (updated_thermal_state[:-2] - center)
    widths = ((0, 0), (1, 1), (0, 0))
    cond_pad = jnp.pad(center_cond, widths)
    heat_pad = jnp.pad(center, widths)
    fluxes = fluxes + face_mean(center_cond, cond_pad[:, 2:]) * (heat_pad[:, 2:] - center)
    fluxes = fluxes + face_mean(center_cond, cond_pad[:, :-2]) * (heat_pad[:, :-2] - center)
    widths = ((0, 0), (0, 0), (1, 1))
    cond_pad = jnp.pad(center_cond, widths)
    heat_pad = jnp.pad(center, widths)
    fluxes = fluxes + face_mean(center_cond, cond_pad[:, :, 2:]) * (heat_pad[:, :, 2:] - center)
    fluxes = fluxes + face_mean(center_cond, cond_pad[:, :, :-2]) * (heat_pad[:, :, :-2] - center)
    return center + coeffs[1:-1] * fluxes


def march(carry, pair):
    keep_row, gain_row = pair
    return keep_row * carry + gain_row, carry


def reference(initial_voxel_degrees, alloy_tag_per_voxel, thermal_conductance_per_alloy, specific_storage_per_alloy, bore_boundary_positions, surface_transfer_coefficient, surface_over_flow_ratio, flow_direction_flag, entry_coolant_degrees):
    conduct = lookup(alloy_tag_per_voxel, thermal_conductance_per_alloy)
    coeffs = 0.16 / lookup(alloy_tag_per_voxel, specific_storage_per_alloy)
    widths = ((1, 1), (0, 0), (0, 0))
    cond_pad = jnp.pad(conduct, widths)
    coeff_pad = jnp.pad(coeffs, widths)
    updated_thermal_state = initial_voxel_degrees
    for repeat in range(STEPS):
        updated_thermal_state = advance(jnp.pad(updated_thermal_state, widths), cond_pad, coeff_pad)
    flat = updated_thermal_state.reshape(-1)
    offsets = (jnp.arange(N_BRICK, dtype=jnp.int32) * (CX * NY * NZ))[:, None, None]
    global_cells = (bore_boundary_positions + offsets).astype(jnp.int32)
    wall_temps = flat[global_cells]
    wall_mean = jnp.mean(wall_temps, axis=2)
    keep = jnp.exp(-surface_over_flow_ratio[None, :] * surface_transfer_coefficient)
    gain = (1.0 - keep) * wall_mean
    _, forward_in = lax.scan(march, entry_coolant_degrees, (keep, gain))
    _, backward_in = lax.scan(march, entry_coolant_degrees, (keep, gain), reverse=True)
    inflow = jnp.where(flow_direction_flag[None, :] == 0, forward_in, backward_in)
    coolant_mid = 0.5 * (inflow + keep * inflow + gain)
    change = 0.5 * (1.0 - keep)[:, :, None] * (coolant_mid[:, :, None] - wall_temps)
    final = flat.at[global_cells.reshape(-1)].add(change.reshape(-1)).reshape(updated_thermal_state.shape)
    return final, coolant_mid
```

```python
import functools

import jax
import jax.numpy as jnp
from jax import lax
from jax.experimental import pallas as pl
from jax.experimental.pallas import tpu as pltpu
from jax.sharding import PartitionSpec as P

STEPS = 3
ROWS = 32
VMEM = pl.BlockSpec(memory_space=pltpu.VMEM)
SMEM = pl.BlockSpec(memory_space=pltpu.SMEM)
LIMIT = 48 * 1024 * 1024


def log2(n):
    return n.bit_length() - 1


def iota(shape, dim):
    return lax.broadcasted_iota(jnp.int32, shape, dim)


def sort_kernel(pos_ref, keys_ref):
    lines, wall = pos_ref.shape
    half = wall // 2
    keys = pos_ref[...] * lines + iota((lines, wall), 0)
    x = jnp.concatenate([keys[:, :half], keys[:, half:]], axis=0)
    shape = x.shape
    row = iota(shape, 0)
    place = (row % lines) * wall + (row // lines) * half + iota(shape, 1)
    total = lines * wall
    for phase in range(1, log2(total) + 1):
        for stage in range(phase - 1, -1, -1):
            step = 1 << stage
            if step < half:
                axis, amount = 1, step
            elif step == half:
                axis, amount = 0, lines
            else:
                axis, amount = 0, step // wall
            size = shape[axis]
            low = (place & step) == 0
            up = pltpu.roll(x, size - amount, axis)
            down = up if 2 * amount == size else pltpu.roll(x, amount, axis)
            other = jnp.where(low, up, down)
            if phase == log2(total):
                take_min = low
            else:
                take_min = ((place >> stage) & 1) == ((place >> phase) & 1)
            x = jnp.where(take_min, jnp.minimum(x, other), jnp.maximum(x, other))
    keys_ref[:, :half] = x[:lines]
    keys_ref[:, half:] = x[lines:]


def pick(tags, table_ref):
    level = [table_ref[i] for i in range(table_ref.shape[0])]
    bit = 0
    while len(level) > 1:
        odd = (tags & (1 << bit)) != 0
        pairs = [level[i : i + 2] for i in range(0, len(level), 2)]
        level = [jnp.where(odd, p[1], p[0]) if len(p) == 2 else p[0] for p in pairs]
        bit += 1
    return level[0]


def face_mean(left, right):
    return 2.0 * left * right / (left + right + 1e-30)


def conduct_kernel(
    count,
    temp_ref, tag_ref, cond_table, store_table, out_ref,
    first, second, cond, coef, gx, gy, gz, temp_halo, tag_halo, send_sem, recv_sem,
):
    nx, ny, nz = temp_ref.shape
    me = lax.axis_index("brick")
    left, right = me - 1, me + 1
    has_left, has_right = me > 0, me < count - 1

    def copy(src, dst, slot, side):
        target = left if side == 0 else right
        return pltpu.make_async_remote_copy(
            src_ref=src,
            dst_ref=dst,
            send_sem=send_sem.at[slot, side],
            recv_sem=recv_sem.at[slot, 1 - side],
            device_id=(lax.axis_index("pour"), target),
            device_id_type=pl.DeviceIdType.MESH,
        )

    def tag_copy(side):
        return copy(tag_ref.at[0 if side == 0 else nx - 1], tag_halo.at[1 - side], STEPS, side)

    def temp_copy(src, step, side):
        return copy(src.at[0 if side == 0 else nx - 1], temp_halo.at[step, 1 - side], step, side)

    sides = ((0, has_left), (1, has_right))
    barrier = pltpu.get_barrier_semaphore()
    for side, present in sides:
        @pl.when(present)
        def _():
            pl.semaphore_signal(
                barrier, inc=1,
                device_id=(lax.axis_index("pour"), left if side == 0 else right),
                device_id_type=pl.DeviceIdType.MESH,
            )
    pl.semaphore_wait(barrier, has_left.astype(jnp.int32) + has_right.astype(jnp.int32))
    for side, present in sides:
        @pl.when(present)
        def _():
            tag_copy(side).start()
            temp_copy(temp_ref, 0, side).start()

        @pl.when(jnp.logical_not(present))
        def _():
            for step in range(STEPS):
                temp_halo[step, side] = jnp.zeros((ny, nz), jnp.float32)

    chunks = [pl.ds(r, ROWS) for r in range(0, ny, ROWS)]
    row = iota((ROWS, nz), 0)
    lane = iota((ROWS, nz), 1)

    def above(ref, plane, r):
        if r:
            return ref[plane, pl.ds(r - 1, ROWS), :]
        here = ref[plane, pl.ds(r, ROWS), :]
        return jnp.where(row == 0, here, pltpu.roll(here, 1, 0))

    def below(ref, plane, r):
        if r + ROWS < ny:
            return ref[plane, pl.ds(r + 1, ROWS), :]
        here = ref[plane, pl.ds(r, ROWS), :]
        return jnp.where(row == ROWS - 1, here, pltpu.roll(here, ROWS - 1, 0))

    def properties(plane, _):
        for rows in chunks:
            tags = tag_ref[plane, rows, :]
            cond[plane, rows, :] = pick(tags, cond_table)
            coef[plane, rows, :] = 0.16 / pick(tags, store_table)
        return 0

    lax.fori_loop(0, nx, properties, 0)

    def faces(plane, _):
        for r, rows in zip(range(0, ny, ROWS), chunks):
            here = cond[plane, rows, :]
            gy[plane, rows, :] = face_mean(here, below(cond, plane, r))
            side = face_mean(here, pltpu.roll(here, nz - 1, 1))
            gz[plane, rows, :] = jnp.where(lane == nz - 1, 0.0, side)
        return 0

    lax.fori_loop(0, nx, faces, 0)

    def faces_x(plane, _):
        for rows in chunks:
            gx[plane, rows, :] = face_mean(cond[plane - 1, rows, :], cond[plane, rows, :])
        return 0

    lax.fori_loop(1, nx, faces_x, 0)

    def update(src, dst, plane, before, after):
        for r, rows in zip(range(0, ny, ROWS), chunks):
            here = src[plane, rows, :]
            flux = gx[plane + 1, rows, :] * (after(rows) - here)
            flux = flux - gx[plane, rows, :] * (here - before(rows))
            flux = flux + gy[plane, rows, :] * (below(src, plane, r) - here)
            flux = flux - above(gy, plane, r) * (here - above(src, plane, r))
            side = gz[plane, rows, :] * (pltpu.roll(here, nz - 1, 1) - here)
            flux = flux + (side - pltpu.roll(side, 1, 1))
            dst[plane, rows, :] = here + coef[plane, rows, :] * flux

    def inner(src, dst):
        def body(plane, _):
            update(
                src, dst, plane,
                lambda rows: src[plane - 1, rows, :],
                lambda rows: src[plane + 1, rows, :],
            )
            return 0

        lax.fori_loop(1, nx - 1, body, 0)

    def outer(src, dst, step):
        for side, present in sides:
            @pl.when(present)
            def _():
                temp_copy(src, step, 1 - side).wait_recv()
        update(src, dst, 0, lambda rows: temp_halo[step, 0, rows, :], lambda rows: src[1, rows, :])
        update(
            src, dst, nx - 1,
            lambda rows: src[nx - 2, rows, :], lambda rows: temp_halo[step, 1, rows, :],
        )
        if step + 1 < STEPS:
            for side, present in sides:
                @pl.when(present)
                def _():
                    temp_copy(dst, step + 1, side).start()

    for side, present in sides:
        outer_face, edge = (0, 0) if side == 0 else (nx, nx - 1)

        @pl.when(present)
        def _():
            tag_copy(1 - side).wait_recv()
            for rows in chunks:
                beyond = pick(tag_halo[side, rows, :], cond_table)
                gx[outer_face, rows, :] = face_mean(beyond, cond[edge, rows, :])

        @pl.when(jnp.logical_not(present))
        def _():
            gx[outer_face] = jnp.zeros((ny, nz), jnp.float32)

    outer(temp_ref, first, 0)
    inner(temp_ref, first)
    inner(first, second)
    outer(first, second, 1)
    inner(second, out_ref)
    outer(second, out_ref, 2)
    for side, present in sides:
        @pl.when(present)
        def _():
            tag_copy(side).wait_send()
            temp_copy(temp_ref, 0, side).wait_send()
            temp_copy(first, 1, side).wait_send()
            temp_copy(second, 2, side).wait_send()


def split(x):
    high = x.astype(jnp.bfloat16)
    return high, (x - high.astype(jnp.float32)).astype(jnp.bfloat16)


def to_row(column):
    n = column.shape[0]
    return jnp.sum(jnp.where(iota((n, n), 0) == iota((n, n), 1), column, 0.0), axis=0, keepdims=True)


def to_column(row):
    n = row.shape[1]
    return jnp.sum(jnp.where(iota((n, n), 0) == iota((n, n), 1), row, 0.0), axis=1, keepdims=True)


def gather_kernel(heat_ref, keys_ref, edge_ref, surf_ref, ratio_ref, wall_ref, coef_ref, high_t, low_t):
    nx, ny, nz = heat_ref.shape
    lines, wall = keys_ref.shape
    line_bits, col_bits, row_bits = log2(lines), log2(nz), log2(ny)
    plane_shift = line_bits + col_bits + row_bits

    def turn(plane, _):
        high_t[plane], low_t[plane] = split(heat_ref[plane].T)
        return 0

    lax.fori_loop(0, nx, turn, 0)

    def block(b, sums):
        key = keys_ref[pl.ds(b, 1), :]
        col = (key >> line_bits) & (nz - 1)
        row = (key >> (line_bits + col_bits)) & (ny - 1)
        plane = key >> plane_shift
        at_col = iota((nz, wall), 0) == col

        def visit(t, acc):
            hit = iota((ny, wall), 0) == jnp.where(plane == t, row, -1)
            hot = jnp.where(hit, 1.0, 0.0).astype(jnp.bfloat16)
            got = jnp.dot(high_t[t], hot, preferred_element_type=jnp.float32)
            got = got + jnp.dot(low_t[t], hot, preferred_element_type=jnp.float32)
            return acc + jnp.sum(jnp.where(at_col, got, 0.0), axis=0, keepdims=True)

        low = edge_ref[b, 0] >> plane_shift
        high = edge_ref[b, wall - 1] >> plane_shift
        temps = lax.fori_loop(low, high + 1, visit, jnp.zeros((1, wall), jnp.float32))
        wall_ref[pl.ds(b, 1), :] = temps
        return sums + jnp.where(iota((lines, wall), 0) == (key & (lines - 1)), temps, 0.0)

    sums = lax.fori_loop(0, lines, block, jnp.zeros((lines, wall), jnp.float32))
    mean = to_row(jnp.sum(sums, axis=1, keepdims=True)) * (1.0 / wall)
    keep = jnp.exp(-ratio_ref[...] * surf_ref[...])
    coef_ref[...] = jnp.zeros(coef_ref.shape, jnp.float32)
    coef_ref[0:1, 0:lines] = keep
    coef_ref[1:2, 0:lines] = (1.0 - keep) * mean


def march_kernel(count, coef_ref, flag_ref, entry_ref, out_ref, every, send_sem, recv_sem):
    lines = flag_ref.shape[1]
    me = lax.axis_index("brick")
    pour = lax.axis_index("pour")

    def copy(offset, place):
        return pltpu.make_async_remote_copy(
            src_ref=coef_ref,
            dst_ref=every.at[place],
            send_sem=send_sem.at[offset],
            recv_sem=recv_sem.at[place],
            device_id=(pour, lax.rem(me + offset, count)),
            device_id_type=pl.DeviceIdType.MESH,
        )

    barrier = pltpu.get_barrier_semaphore()

    def greet(offset, _):
        pl.semaphore_signal(
            barrier, inc=1,
            device_id=(pour, lax.rem(me + offset, count)),
            device_id_type=pl.DeviceIdType.MESH,
        )
        return 0

    lax.fori_loop(1, count, greet, 0)
    pl.semaphore_wait(barrier, count - 1)

    def send(offset, _):
        copy(offset, me).start()
        return 0

    lax.fori_loop(1, count, send, 0)
    every[me] = coef_ref[...]

    def arrive(offset, _):
        copy(offset, lax.rem(me + offset, count)).wait_recv()
        return 0

    lax.fori_loop(1, count, arrive, 0)

    def flow(place, inflow):
        pair = every[place]
        return pair[0:1, 0:lines] * inflow + pair[1:2, 0:lines]

    entry = entry_ref[...]
    forward = lax.fori_loop(0, me, flow, entry)
    last = count - 1
    backward = lax.fori_loop(0, last - me, lambda i, x: flow(last - i, x), entry)
    inflow = jnp.where(flag_ref[...] == 0, forward, backward)
    keep, gain = coef_ref[0:1, 0:lines], coef_ref[1:2, 0:lines]
    out_ref[...] = 0.5 * (inflow + keep * inflow + gain)

    def sent(offset, _):
        copy(offset, me).wait_send()
        return 0

    lax.fori_loop(1, count, sent, 0)


def scatter_kernel(heat_ref, keys_ref, edge_ref, wall_ref, coef_ref, cool_ref, out_ref):
    nx, ny, nz = heat_ref.shape
    lines, wall = keys_ref.shape
    line_bits, col_bits, row_bits = log2(lines), log2(nz), log2(ny)
    plane_shift = line_bits + col_bits + row_bits
    share = to_column(0.5 * (1.0 - coef_ref[0:1, 0:lines]))
    cool = to_column(cool_ref[...])

    def start(plane, _):
        out_ref[plane] = heat_ref[plane]
        return 0

    lax.fori_loop(0, nx, start, 0)

    def block(b, _):
        key = keys_ref[pl.ds(b, 1), :]
        col = (key >> line_bits) & (nz - 1)
        row = (key >> (line_bits + col_bits)) & (ny - 1)
        plane = key >> plane_shift
        mine = iota((lines, wall), 0) == (key & (lines - 1))
        share_row = jnp.sum(jnp.where(mine, share, 0.0), axis=0, keepdims=True)
        cool_row = jnp.sum(jnp.where(mine, cool, 0.0), axis=0, keepdims=True)
        change = share_row * (cool_row - wall_ref[pl.ds(b, 1), :])
        at_col = iota((nz, wall), 0) == col
        high, low = split(change)
        high = jnp.where(at_col, high.astype(jnp.float32), 0.0).astype(jnp.bfloat16)
        low = jnp.where(at_col, low.astype(jnp.float32), 0.0).astype(jnp.bfloat16)

        def visit(t, _):
            hit = iota((ny, wall), 0) == jnp.where(plane == t, row, -1)
            hot = jnp.where(hit, 1.0, 0.0).astype(jnp.bfloat16)
            dims = (((1,), (1,)), ((), ()))
            add = lax.dot_general(hot, high, dims, preferred_element_type=jnp.float32)
            add = add + lax.dot_general(hot, low, dims, preferred_element_type=jnp.float32)
            out_ref[t] = out_ref[t] + add
            return 0

        first = edge_ref[b, 0] >> plane_shift
        last = edge_ref[b, wall - 1] >> plane_shift
        lax.fori_loop(first, last + 1, visit, 0)
        return 0

    lax.fori_loop(0, lines, block, 0)


def per_device(count, temp, tags, cond_table, store_table, pos, surf, ratio, flag, entry):
    nx, ny, nz = temp.shape
    f32 = jnp.float32
    lines, wall = pos.shape[1:]
    pos, ratio, flag, entry = pos[0], ratio[None], flag[None], entry[None]
    local = pltpu.CompilerParams(vmem_limit_bytes=LIMIT)
    keys = pl.pallas_call(
        sort_kernel,
        out_shape=jax.ShapeDtypeStruct((lines, wall), jnp.int32),
        in_specs=[VMEM],
        out_specs=VMEM,
        compiler_params=local,
        name="sort",
    )(pos)
    brick = (nx, ny, nz)
    heated = pl.pallas_call(
        functools.partial(conduct_kernel, count),
        out_shape=jax.ShapeDtypeStruct(brick, f32),
        in_specs=[VMEM, VMEM, SMEM, SMEM],
        out_specs=VMEM,
        scratch_shapes=[
            pltpu.VMEM(brick, f32),
            pltpu.VMEM(brick, f32),
            pltpu.VMEM(brick, f32),
            pltpu.VMEM(brick, f32),
            pltpu.VMEM((nx + 1, ny, nz), f32),
            pltpu.VMEM(brick, f32),
            pltpu.VMEM(brick, f32),
            pltpu.VMEM((STEPS, 2, ny, nz), f32),
            pltpu.VMEM((2, ny, nz), jnp.int32),
            pltpu.SemaphoreType.DMA((STEPS + 1, 2)),
            pltpu.SemaphoreType.DMA((STEPS + 1, 2)),
        ],
        compiler_params=pltpu.CompilerParams(
            vmem_limit_bytes=LIMIT, collective_id=0, has_side_effects=True
        ),
        name="conduct",
    )(temp, tags, cond_table, store_table)
    walls, coef = pl.pallas_call(
        gather_kernel,
        out_shape=(
            jax.ShapeDtypeStruct((lines, wall), f32),
            jax.ShapeDtypeStruct((8, 128), f32),
        ),
        in_specs=[VMEM, VMEM, SMEM, VMEM, VMEM],
        out_specs=(VMEM, VMEM),
        scratch_shapes=[
            pltpu.VMEM((nx, nz, ny), jnp.bfloat16),
            pltpu.VMEM((nx, nz, ny), jnp.bfloat16),
        ],
        compiler_params=local,
        name="gather",
    )(heated, keys, keys, surf, ratio)
    cool = pl.pallas_call(
        functools.partial(march_kernel, count),
        out_shape=jax.ShapeDtypeStruct((1, lines), f32),
        in_specs=[VMEM, VMEM, VMEM],
        out_specs=VMEM,
        scratch_shapes=[
            pltpu.VMEM((count, 8, 128), f32),
            pltpu.SemaphoreType.DMA((count,)),
            pltpu.SemaphoreType.DMA((count,)),
        ],
        compiler_params=pltpu.CompilerParams(collective_id=1, has_side_effects=True),
        name="march",
    )(coef, flag, entry)
    final = pl.pallas_call(
        scatter_kernel,
        out_shape=jax.ShapeDtypeStruct(brick, f32),
        in_specs=[VMEM, VMEM, SMEM, VMEM, VMEM, VMEM],
        out_specs=VMEM,
        compiler_params=local,
        name="scatter",
    )(heated, keys, keys, walls, coef, cool)
    return final, cool


def solution(mesh):
    return jax.shard_map(
        functools.partial(per_device, mesh.shape["brick"]),
        mesh=mesh,
        in_specs=(
            P(("pour", "brick"), None, None),
            P("brick", None, None),
            P(),
            P(),
            P("brick", None, None),
            P("brick", None),
            P(),
            P(),
            P("pour"),
        ),
        out_specs=(P(("pour", "brick"), None, None), P(("pour", "brick"), None)),
        check_vma=False,
    )
```

```python
import functools

import jax
import jax.numpy as jnp
from jax import lax
from jax.experimental import pallas as pl
from jax.experimental.pallas import tpu as pltpu
from jax.sharding import PartitionSpec as P

STEPS = 3
ROWS = 32
GROUP = 4
VMEM = pl.BlockSpec(memory_space=pltpu.VMEM)
ANY = pl.BlockSpec(memory_space=pl.ANY)
LIMIT = 48 * 1024 * 1024


def log2(n):
    return n.bit_length() - 1


def iota(shape, dim):
    return lax.broadcasted_iota(jnp.int32, shape, dim)


def sort_keys(pos_ref, keys_ref):
    lines, wall = pos_ref.shape
    half = wall // 2
    keys = pos_ref[...] * lines + iota((lines, wall), 0)
    x = jnp.concatenate([keys[:, :half], keys[:, half:]], axis=0)
    shape = x.shape
    row = iota(shape, 0)
    place = (row % lines) * wall + (row // lines) * half + iota(shape, 1)
    total = lines * wall
    for phase in range(1, log2(total) + 1):
        for stage in range(phase - 1, -1, -1):
            step = 1 << stage
            if step < half:
                axis, amount = 1, step
            elif step == half:
                axis, amount = 0, lines
            else:
                axis, amount = 0, step // wall
            size = shape[axis]
            low = (place & step) == 0
            up = pltpu.roll(x, size - amount, axis)
            down = up if 2 * amount == size else pltpu.roll(x, amount, axis)
            other = jnp.where(low, up, down)
            if phase == log2(total):
                take_min = low
            else:
                take_min = ((place >> stage) & 1) == ((place >> phase) & 1)
            x = jnp.where(take_min, jnp.minimum(x, other), jnp.maximum(x, other))
    keys_ref[:, :half] = x[:lines]
    keys_ref[:, half:] = x[lines:]


def pick(tags, table_ref):
    level = [table_ref[i] for i in range(table_ref.shape[0])]
    bit = 0
    while len(level) > 1:
        odd = (tags & (1 << bit)) != 0
        pairs = [level[i : i + 2] for i in range(0, len(level), 2)]
        level = [jnp.where(odd, p[1], p[0]) if len(p) == 2 else p[0] for p in pairs]
        bit += 1
    return level[0]


def inverse(x):
    guess = pl.reciprocal(x, approx=True)
    guess = guess * (2.0 - x * guess)
    return guess * (2.0 - x * guess)


def face_mean(left, right):
    return 2.0 * left * right * inverse(left + right + 1e-30)


def conduct_kernel(
    count,
    temp_hbm, tag_hbm, cond_hbm, store_hbm, pos_ref, out_ref, keys_ref,
    temp_ref, tag_ref, cond_table, store_table,
    first, second, cond, coef, gx, gy, gz, temp_halo, tag_halo, send_sem, recv_sem, local_sem,
):
    nx, ny, nz = temp_ref.shape
    loads = [
        pltpu.make_async_copy(src, dst, local_sem.at[i])
        for i, (src, dst) in enumerate(
            [
                (tag_hbm, tag_ref),
                (cond_hbm, cond_table),
                (store_hbm, store_table),
                (temp_hbm, temp_ref),
            ]
        )
    ]
    for load in loads:
        load.start()
    me = lax.axis_index("brick")
    left, right = me - 1, me + 1
    has_left, has_right = me > 0, me < count - 1

    def copy(src, dst, slot, side):
        target = left if side == 0 else right
        return pltpu.make_async_remote_copy(
            src_ref=src,
            dst_ref=dst,
            send_sem=send_sem.at[slot, side],
            recv_sem=recv_sem.at[slot, 1 - side],
            device_id=(lax.axis_index("pour"), target),
            device_id_type=pl.DeviceIdType.MESH,
        )

    def tag_copy(side):
        return copy(tag_hbm.at[0 if side == 0 else nx - 1], tag_halo.at[1 - side], STEPS, side)

    def temp_copy(src, step, side):
        return copy(src.at[0 if side == 0 else nx - 1], temp_halo.at[step, 1 - side], step, side)

    sides = ((0, has_left), (1, has_right))
    barrier = pltpu.get_barrier_semaphore()
    for side, present in sides:
        @pl.when(present)
        def _():
            pl.semaphore_signal(
                barrier, inc=1,
                device_id=(lax.axis_index("pour"), left if side == 0 else right),
                device_id_type=pl.DeviceIdType.MESH,
            )
    pl.semaphore_wait(barrier, has_left.astype(jnp.int32) + has_right.astype(jnp.int32))
    for side, present in sides:
        @pl.when(present)
        def _():
            tag_copy(side).start()
            temp_copy(temp_hbm, 0, side).start()

        @pl.when(jnp.logical_not(present))
        def _():
            for step in range(STEPS):
                temp_halo[step, side] = jnp.zeros((ny, nz), jnp.float32)

    sort_keys(pos_ref, keys_ref)
    for load in loads:
        load.wait()

    chunks = [pl.ds(r, ROWS) for r in range(0, ny, ROWS)]
    row = iota((ROWS, nz), 0)
    lane = iota((ROWS, nz), 1)

    def below(ref, plane, r):
        if r + ROWS < ny:
            return ref[plane, pl.ds(r + 1, ROWS), :]
        here = ref[plane, pl.ds(r, ROWS), :]
        return jnp.where(row == ROWS - 1, here, pltpu.roll(here, ROWS - 1, 0))

    def properties(plane, _):
        for rows in chunks:
            tags = tag_ref[plane, rows, :]
            cond[plane, rows, :] = pick(tags, cond_table)
            coef[plane, rows, :] = 0.16 * inverse(pick(tags, store_table))
        return 0

    lax.fori_loop(0, nx, properties, 0)

    def faces(plane, _):
        for r, rows in zip(range(0, ny, ROWS), chunks):
            here = cond[plane, rows, :]
            gy[plane, rows, :] = face_mean(here, below(cond, plane, r))
            side = face_mean(here, pltpu.roll(here, nz - 1, 1))
            gz[plane, rows, :] = jnp.where(lane == nz - 1, 0.0, side)
        return 0

    lax.fori_loop(0, nx, faces, 0)

    def faces_x(plane, _):
        for rows in chunks:
            gx[plane, rows, :] = face_mean(cond[plane - 1, rows, :], cond[plane, rows, :])
        return 0

    lax.fori_loop(1, nx, faces_x, 0)

    def update(src, dst, plane, before, after):
        last = jnp.zeros((8, nz), jnp.float32)
        for r, rows in zip(range(0, ny, ROWS), chunks):
            here = src[plane, rows, :]
            flux = gx[plane + 1, rows, :] * (after(rows) - here)
            flux = flux - gx[plane, rows, :] * (here - before(rows))
            side = gy[plane, rows, :] * (below(src, plane, r) - here)
            turned = pltpu.roll(side, 1, 0)
            top = jnp.where(row[:8] == 0, last, turned[:8])
            last = turned[:8]
            flux = flux + (side - jnp.concatenate([top, turned[8:]], axis=0))
            side = gz[plane, rows, :] * (pltpu.roll(here, nz - 1, 1) - here)
            flux = flux + (side - pltpu.roll(side, 1, 1))
            dst[plane, rows, :] = here + coef[plane, rows, :] * flux

    def inner(src, dst):
        def body(plane, _):
            update(
                src, dst, plane,
                lambda rows: src[plane - 1, rows, :],
                lambda rows: src[plane + 1, rows, :],
            )
            return 0

        lax.fori_loop(1, nx - 1, body, 0)

    def outer(src, dst, step):
        for side, present in sides:
            @pl.when(present)
            def _():
                temp_copy(src, step, 1 - side).wait_recv()
        update(src, dst, 0, lambda rows: temp_halo[step, 0, rows, :], lambda rows: src[1, rows, :])
        update(
            src, dst, nx - 1,
            lambda rows: src[nx - 2, rows, :], lambda rows: temp_halo[step, 1, rows, :],
        )
        if step + 1 < STEPS:
            for side, present in sides:
                @pl.when(present)
                def _():
                    temp_copy(dst, step + 1, side).start()

    for side, present in sides:
        outer_face, edge = (0, 0) if side == 0 else (nx, nx - 1)

        @pl.when(present)
        def _():
            tag_copy(1 - side).wait_recv()
            for rows in chunks:
                beyond = pick(tag_halo[side, rows, :], cond_table)
                gx[outer_face, rows, :] = face_mean(beyond, cond[edge, rows, :])

        @pl.when(jnp.logical_not(present))
        def _():
            gx[outer_face] = jnp.zeros((ny, nz), jnp.float32)

    outer(temp_ref, first, 0)
    inner(temp_ref, first)
    inner(first, second)
    outer(first, second, 1)
    inner(second, out_ref)
    outer(second, out_ref, 2)
    for side, present in sides:
        @pl.when(present)
        def _():
            tag_copy(side).wait_send()
            temp_copy(temp_hbm, 0, side).wait_send()
            temp_copy(first, 1, side).wait_send()
            temp_copy(second, 2, side).wait_send()


def split(x):
    high = x.astype(jnp.bfloat16)
    return high, (x - high.astype(jnp.float32)).astype(jnp.bfloat16)


def to_row(column):
    n = column.shape[0]
    return jnp.sum(jnp.where(iota((n, n), 0) == iota((n, n), 1), column, 0.0), axis=0, keepdims=True)


def to_column(row):
    n = row.shape[1]
    return jnp.sum(jnp.where(iota((n, n), 0) == iota((n, n), 1), row, 0.0), axis=1, keepdims=True)


def fields(key, lines, ny, nz):
    shift = log2(lines)
    col = (key >> shift) & (nz - 1)
    row = (key >> (shift + log2(nz))) & (ny - 1)
    return key & (lines - 1), col, row, key >> (shift + log2(nz) + log2(ny))


def hot_rows(plane, t, row, ny):
    hit = iota((ny, row.shape[1]), 0) == jnp.where(plane == t, row, -1)
    return jnp.where(hit, 1.0, 0.0).astype(jnp.bfloat16)


def gather_kernel(
    heat_ref, keys_ref, surf_ref, ratio_ref, wall_ref, coef_ref, pieces, edge_ref, edge_sem
):
    nx, ny, nz = heat_ref.shape
    lines, wall = keys_ref.shape
    plane_shift = log2(lines) + log2(nz) + log2(ny)
    load = pltpu.make_async_copy(keys_ref, edge_ref, edge_sem)
    load.start()

    def turn(plane, _):
        high, low = split(heat_ref[plane].T)
        pieces[plane, :nz] = high
        pieces[plane, nz:] = low
        return 0

    lax.fori_loop(0, nx, turn, 0)
    load.wait()

    def visit(b, t):
        line, col, row, plane = fields(keys_ref[pl.ds(b, 1), :], lines, ny, nz)
        hot = hot_rows(plane, t, row, ny)
        got = jnp.dot(pieces[t], hot, preferred_element_type=jnp.float32)
        at_col = iota((nz, wall), 0) == col
        return jnp.sum(jnp.where(at_col, got[:nz] + got[nz:], 0.0), axis=0, keepdims=True)

    def blocks(group, _):
        for i in range(GROUP):
            b = group * GROUP + i
            wall_ref[pl.ds(b, 1), :] = visit(b, edge_ref[b, 0] >> plane_shift)
        return 0

    lax.fori_loop(0, lines // GROUP, blocks, 0)

    def rest(b, _):
        def more(t, _):
            wall_ref[pl.ds(b, 1), :] = wall_ref[pl.ds(b, 1), :] + visit(b, t)
            return 0

        low = edge_ref[b, 0] >> plane_shift
        lax.fori_loop(low + 1, (edge_ref[b, wall - 1] >> plane_shift) + 1, more, 0)
        return 0

    lax.fori_loop(0, lines, rest, 0)

    sums = jnp.zeros((lines, wall), jnp.float32)
    for b in range(lines):
        line = keys_ref[b : b + 1, :] & (lines - 1)
        sums = sums + jnp.where(iota((lines, wall), 0) == line, wall_ref[b : b + 1, :], 0.0)
    mean = to_row(jnp.sum(sums, axis=1, keepdims=True)) * (1.0 / wall)
    keep = jnp.exp(-ratio_ref[...] * surf_ref[...])
    coef_ref[...] = jnp.zeros(coef_ref.shape, jnp.float32)
    coef_ref[0:1, 0:lines] = keep
    coef_ref[1:2, 0:lines] = (1.0 - keep) * mean


def march_kernel(count, coef_ref, flag_ref, entry_ref, out_ref, every, send_sem, recv_sem):
    lines = flag_ref.shape[1]
    me = lax.axis_index("brick")
    pour = lax.axis_index("pour")

    def copy(offset, place):
        return pltpu.make_async_remote_copy(
            src_ref=coef_ref,
            dst_ref=every.at[place],
            send_sem=send_sem.at[offset],
            recv_sem=recv_sem.at[place],
            device_id=(pour, lax.rem(me + offset, count)),
            device_id_type=pl.DeviceIdType.MESH,
        )

    barrier = pltpu.get_barrier_semaphore()

    def greet(offset, _):
        pl.semaphore_signal(
            barrier, inc=1,
            device_id=(pour, lax.rem(me + offset, count)),
            device_id_type=pl.DeviceIdType.MESH,
        )
        return 0

    lax.fori_loop(1, count, greet, 0)
    pl.semaphore_wait(barrier, count - 1)

    def send(offset, _):
        copy(offset, me).start()
        return 0

    lax.fori_loop(1, count, send, 0)
    every[me] = coef_ref[...]

    def arrive(offset, _):
        copy(offset, lax.rem(me + offset, count)).wait_recv()
        return 0

    lax.fori_loop(1, count, arrive, 0)

    last = count - 1

    def flow(i, inflows):
        forward, backward = inflows
        up, down = every[i], every[last - i]
        forth = up[0:1, 0:lines] * forward + up[1:2, 0:lines]
        back = down[0:1, 0:lines] * backward + down[1:2, 0:lines]
        return jnp.where(i < me, forth, forward), jnp.where(last - i > me, back, backward)

    entry = entry_ref[...]
    forward, backward = lax.fori_loop(0, last, flow, (entry, entry), unroll=5)
    inflow = jnp.where(flag_ref[...] == 0, forward, backward)
    keep, gain = coef_ref[0:1, 0:lines], coef_ref[1:2, 0:lines]
    out_ref[...] = 0.5 * (inflow + keep * inflow + gain)

    def sent(offset, _):
        copy(offset, me).wait_send()
        return 0

    lax.fori_loop(1, count, sent, 0)


def scatter_kernel(
    heat_ref, keys_ref, wall_ref, coef_ref, cool_ref, out_ref, edge_ref, edge_sem
):
    nx, ny, nz = heat_ref.shape
    lines, wall = keys_ref.shape
    plane_shift = log2(lines) + log2(nz) + log2(ny)
    load = pltpu.make_async_copy(keys_ref, edge_ref, edge_sem)
    load.start()
    share = to_column(0.5 * (1.0 - coef_ref[0:1, 0:lines]))
    cool = to_column(cool_ref[...])

    def start(plane, _):
        out_ref[plane] = heat_ref[plane]
        return 0

    lax.fori_loop(0, nx, start, 0)
    load.wait()

    def visit(b, t):
        line, col, row, plane = fields(keys_ref[pl.ds(b, 1), :], lines, ny, nz)
        mine = iota((lines, wall), 0) == line
        share_row = jnp.sum(jnp.where(mine, share, 0.0), axis=0, keepdims=True)
        cool_row = jnp.sum(jnp.where(mine, cool, 0.0), axis=0, keepdims=True)
        high, low = split(share_row * (cool_row - wall_ref[pl.ds(b, 1), :]))
        at_col = iota((nz, wall), 0) == col
        parts = [
            jnp.where(at_col, part.astype(jnp.float32), 0.0).astype(jnp.bfloat16)
            for part in (high, low)
        ]
        hot = hot_rows(plane, t, row, ny)
        return lax.dot_general(
            jnp.concatenate([hot, hot], axis=1),
            jnp.concatenate(parts, axis=1),
            (((1,), (1,)), ((), ())),
            preferred_element_type=jnp.float32,
        )

    def blocks(group, _):
        places = [group * GROUP + i for i in range(GROUP)]
        planes = [edge_ref[b, 0] >> plane_shift for b in places]
        adds = [visit(b, t) for b, t in zip(places, planes)]
        for t, add in zip(planes, adds):
            out_ref[t] = out_ref[t] + add
        return 0

    lax.fori_loop(0, lines // GROUP, blocks, 0)

    def rest(b, _):
        def more(t, _):
            out_ref[t] = out_ref[t] + visit(b, t)
            return 0

        low = edge_ref[b, 0] >> plane_shift
        lax.fori_loop(low + 1, (edge_ref[b, wall - 1] >> plane_shift) + 1, more, 0)
        return 0

    lax.fori_loop(0, lines, rest, 0)


def per_device(count, temp, tags, cond_table, store_table, pos, surf, ratio, flag, entry):
    nx, ny, nz = temp.shape
    f32 = jnp.float32
    lines, wall = pos.shape[1:]
    pos, ratio, flag, entry = pos[0], ratio[None], flag[None], entry[None]
    local = pltpu.CompilerParams(vmem_limit_bytes=LIMIT)
    brick = (nx, ny, nz)
    heated, keys = pl.pallas_call(
        functools.partial(conduct_kernel, count),
        out_shape=(
            jax.ShapeDtypeStruct(brick, f32),
            jax.ShapeDtypeStruct((lines, wall), jnp.int32),
        ),
        in_specs=[ANY, ANY, ANY, ANY, VMEM],
        out_specs=(VMEM, VMEM),
        scratch_shapes=[
            pltpu.VMEM(brick, f32),
            pltpu.VMEM(brick, jnp.int32),
            pltpu.SMEM(cond_table.shape, f32),
            pltpu.SMEM(store_table.shape, f32),
            pltpu.VMEM(brick, f32),
            pltpu.VMEM(brick, f32),
            pltpu.VMEM(brick, f32),
            pltpu.VMEM(brick, f32),
            pltpu.VMEM((nx + 1, ny, nz), f32),
            pltpu.VMEM(brick, f32),
            pltpu.VMEM(brick, f32),
            pltpu.VMEM((STEPS, 2, ny, nz), f32),
            pltpu.VMEM((2, ny, nz), jnp.int32),
            pltpu.SemaphoreType.DMA((STEPS + 1, 2)),
            pltpu.SemaphoreType.DMA((STEPS + 1, 2)),
            pltpu.SemaphoreType.DMA((4,)),
        ],
        compiler_params=pltpu.CompilerParams(
            vmem_limit_bytes=LIMIT, collective_id=0, has_side_effects=True
        ),
        name="conduct",
    )(temp, tags, cond_table, store_table, pos)
    walls, coef = pl.pallas_call(
        gather_kernel,
        out_shape=(
            jax.ShapeDtypeStruct((lines, wall), f32),
            jax.ShapeDtypeStruct((2, 128), f32),
        ),
        in_specs=[VMEM, VMEM, VMEM, VMEM],
        out_specs=(VMEM, VMEM),
        scratch_shapes=[
            pltpu.VMEM((nx, 2 * nz, ny), jnp.bfloat16),
            pltpu.SMEM((lines, wall), jnp.int32),
            pltpu.SemaphoreType.DMA,
        ],
        compiler_params=local,
        name="gather",
    )(heated, keys, surf, ratio)
    cool = pl.pallas_call(
        functools.partial(march_kernel, count),
        out_shape=jax.ShapeDtypeStruct((1, lines), f32),
        in_specs=[VMEM, VMEM, VMEM],
        out_specs=VMEM,
        scratch_shapes=[
            pltpu.VMEM((count, 2, 128), f32),
            pltpu.SemaphoreType.DMA((count,)),
            pltpu.SemaphoreType.DMA((count,)),
        ],
        compiler_params=pltpu.CompilerParams(collective_id=1, has_side_effects=True),
        name="march",
    )(coef, flag, entry)
    final = pl.pallas_call(
        scatter_kernel,
        out_shape=jax.ShapeDtypeStruct(brick, f32),
        in_specs=[VMEM, VMEM, VMEM, VMEM, VMEM],
        out_specs=VMEM,
        scratch_shapes=[
            pltpu.SMEM((lines, wall), jnp.int32),
            pltpu.SemaphoreType.DMA,
        ],
        compiler_params=local,
        name="scatter",
    )(heated, keys, walls, coef, cool)
    return final, cool


def solution(mesh):
    return jax.shard_map(
        functools.partial(per_device, mesh.shape["brick"]),
        mesh=mesh,
        in_specs=(
            P(("pour", "brick"), None, None),
            P("brick", None, None),
            P(),
            P(),
            P("brick", None, None),
            P("brick", None),
            P(),
            P(),
            P("pour"),
        ),
        out_specs=(P(("pour", "brick"), None, None), P(("pour", "brick"), None)),
        check_vma=False,
    )
```

```python
import functools

import jax
import jax.numpy as jnp
from jax import lax
from jax.experimental import pallas as pl
from jax.experimental.pallas import tpu as pltpu
from jax.sharding import PartitionSpec as P

STEPS = 3
ROWS = 32
GROUP = 8
VMEM = pl.BlockSpec(memory_space=pltpu.VMEM)
HBM = pl.BlockSpec(memory_space=pltpu.HBM)
LIMIT = 48 * 1024 * 1024


def log2(n):
    return n.bit_length() - 1


def iota(shape, dim):
    return lax.broadcasted_iota(jnp.int32, shape, dim)


def start_keys(pos_ref):
    lines, wall = pos_ref.shape
    half = wall // 2
    keys = pos_ref[...] * lines + iota((lines, wall), 0)
    return jnp.concatenate([keys[:, :half], keys[:, half:]], axis=0)


def sort_phases(x, first, last):
    half = x.shape[1]
    lines, wall = x.shape[0] // 2, 2 * half
    shape = x.shape
    row = iota(shape, 0)
    place = (row % lines) * wall + (row // lines) * half + iota(shape, 1)
    total = lines * wall
    for phase in range(first, last + 1):
        for stage in range(phase - 1, -1, -1):
            step = 1 << stage
            if step < half:
                axis, amount = 1, step
            elif step == half:
                axis, amount = 0, lines
            else:
                axis, amount = 0, step // wall
            size = shape[axis]
            low = (place & step) == 0
            up = pltpu.roll(x, size - amount, axis)
            down = up if 2 * amount == size else pltpu.roll(x, amount, axis)
            other = jnp.where(low, up, down)
            if phase == log2(total):
                take_min = low
            else:
                take_min = ((place >> stage) & 1) == ((place >> phase) & 1)
            x = jnp.where(take_min, jnp.minimum(x, other), jnp.maximum(x, other))
    return x


def pick(tags, table_ref):
    level = [table_ref[i] for i in range(table_ref.shape[0])]
    bit = 0
    while len(level) > 1:
        odd = (tags & (1 << bit)) != 0
        pairs = [level[i : i + 2] for i in range(0, len(level), 2)]
        level = [jnp.where(odd, p[1], p[0]) if len(p) == 2 else p[0] for p in pairs]
        bit += 1
    return level[0]


def inverse(x):
    guess = pl.reciprocal(x, approx=True)
    guess = guess * (2.0 - x * guess)
    return guess * (2.0 - x * guess)


def face_mean(left, right):
    return 2.0 * left * right * inverse(left + right + 1e-30)


def conduct_kernel(
    count,
    temp_hbm, tag_hbm, cond_hbm, store_hbm, pos_hbm, out_ref, keys_ref,
    pos_ref, temp_ref, tag_ref, cond_table, store_table,
    first, second, cond, coef, gx, gy, gz, temp_halo, tag_halo, send_sem, recv_sem, local_sem,
):
    nx, ny, nz = temp_ref.shape
    loads = [
        pltpu.make_async_copy(src, dst, local_sem.at[i])
        for i, (src, dst) in enumerate(
            [
                (tag_hbm, tag_ref),
                (cond_hbm, cond_table),
                (store_hbm, store_table),
                (temp_hbm, temp_ref),
                (pos_hbm, pos_ref),
            ]
        )
    ]
    for load in loads:
        load.start()
    me = lax.axis_index("brick")
    left, right = me - 1, me + 1
    has_left, has_right = me > 0, me < count - 1

    def copy(src, dst, slot, side):
        target = left if side == 0 else right
        return pltpu.make_async_remote_copy(
            src_ref=src,
            dst_ref=dst,
            send_sem=send_sem.at[slot, side],
            recv_sem=recv_sem.at[slot, 1 - side],
            device_id=(lax.axis_index("pour"), target),
            device_id_type=pl.DeviceIdType.MESH,
        )

    def tag_copy(side):
        return copy(tag_hbm.at[0 if side == 0 else nx - 1], tag_halo.at[1 - side], STEPS, side)

    def temp_copy(src, step, side):
        return copy(src.at[0 if side == 0 else nx - 1], temp_halo.at[step, 1 - side], step, side)

    sides = ((0, has_left), (1, has_right))
    barrier = pltpu.get_barrier_semaphore()
    for side, present in sides:
        @pl.when(present)
        def _():
            pl.semaphore_signal(
                barrier, inc=1,
                device_id=(lax.axis_index("pour"), left if side == 0 else right),
                device_id_type=pl.DeviceIdType.MESH,
            )
    pl.semaphore_wait(barrier, has_left.astype(jnp.int32) + has_right.astype(jnp.int32))
    for side, present in sides:
        @pl.when(present)
        def _():
            tag_copy(side).start()
            temp_copy(temp_hbm, 0, side).start()

        @pl.when(jnp.logical_not(present))
        def _():
            for step in range(STEPS):
                temp_halo[step, side] = jnp.zeros((ny, nz), jnp.float32)

    for load in loads:
        load.wait()

    chunks = [pl.ds(r, ROWS) for r in range(0, ny, ROWS)]
    row = iota((ROWS, nz), 0)
    lane = iota((ROWS, nz), 1)

    def below(ref, plane, r):
        if r + ROWS < ny:
            return ref[plane, pl.ds(r + 1, ROWS), :]
        here = ref[plane, pl.ds(r, ROWS), :]
        return jnp.where(row == ROWS - 1, here, pltpu.roll(here, ROWS - 1, 0))

    def properties(plane, _):
        for rows in chunks:
            tags = tag_ref[plane, rows, :]
            cond[plane, rows, :] = pick(tags, cond_table)
            coef[plane, rows, :] = 0.16 * inverse(pick(tags, store_table))
        return 0

    lax.fori_loop(0, nx, properties, 0)

    def faces(plane, _):
        for r, rows in zip(range(0, ny, ROWS), chunks):
            here = cond[plane, rows, :]
            gy[plane, rows, :] = face_mean(here, below(cond, plane, r))
            side = face_mean(here, pltpu.roll(here, nz - 1, 1))
            gz[plane, rows, :] = jnp.where(lane == nz - 1, 0.0, side)
        return 0

    lax.fori_loop(0, nx, faces, 0)

    def faces_x(plane, _):
        for rows in chunks:
            gx[plane, rows, :] = face_mean(cond[plane - 1, rows, :], cond[plane, rows, :])
        return 0

    lax.fori_loop(1, nx, faces_x, 0)

    def update(src, dst, plane, before, after):
        last = jnp.zeros((8, nz), jnp.float32)
        for r, rows in zip(range(0, ny, ROWS), chunks):
            here = src[plane, rows, :]
            flux = gx[plane + 1, rows, :] * (after(rows) - here)
            flux = flux - gx[plane, rows, :] * (here - before(rows))
            side = gy[plane, rows, :] * (below(src, plane, r) - here)
            turned = pltpu.roll(side, 1, 0)
            top = jnp.where(row[:8] == 0, last, turned[:8])
            last = turned[:8]
            flux = flux + (side - jnp.concatenate([top, turned[8:]], axis=0))
            side = gz[plane, rows, :] * (pltpu.roll(here, nz - 1, 1) - here)
            flux = flux + (side - pltpu.roll(side, 1, 1))
            dst[plane, rows, :] = here + coef[plane, rows, :] * flux

    def inner(src, dst, first_plane, last_plane):
        def body(plane, _):
            update(
                src, dst, plane,
                lambda rows: src[plane - 1, rows, :],
                lambda rows: src[plane + 1, rows, :],
            )
            return 0

        lax.fori_loop(first_plane, last_plane + 1, body, 0)

    def pair(src, dst, plane):
        inner(src, dst, plane, plane)
        inner(src, dst, nx - 1 - plane, nx - 1 - plane)

    def outer(src, dst, step):
        for side, present in sides:
            @pl.when(present)
            def _():
                temp_copy(src, step, 1 - side).wait_recv()

            if side == 0:
                update(
                    src, dst, 0,
                    lambda rows: temp_halo[step, 0, rows, :], lambda rows: src[1, rows, :],
                )
            else:
                update(
                    src, dst, nx - 1,
                    lambda rows: src[nx - 2, rows, :], lambda rows: temp_halo[step, 1, rows, :],
                )
            if step + 1 < STEPS:
                @pl.when(present)
                def _():
                    temp_copy(dst, step + 1, side).start()

    inner(temp_ref, first, 1, nx - 2)
    inner(first, second, 2, nx - 3)
    inner(second, out_ref, 3, nx - 4)

    for side, present in sides:
        outer_face, edge = (0, 0) if side == 0 else (nx, nx - 1)

        @pl.when(present)
        def _():
            tag_copy(1 - side).wait_recv()
            for rows in chunks:
                beyond = pick(tag_halo[side, rows, :], cond_table)
                gx[outer_face, rows, :] = face_mean(beyond, cond[edge, rows, :])

        @pl.when(jnp.logical_not(present))
        def _():
            gx[outer_face] = jnp.zeros((ny, nz), jnp.float32)

    lines, wall = pos_ref.shape
    half = wall // 2
    phases = log2(lines * wall)
    outer(temp_ref, first, 0)
    pair(first, second, 1)
    pair(second, out_ref, 2)
    order = sort_phases(start_keys(pos_ref), 1, phases - 4)
    outer(first, second, 1)
    pair(second, out_ref, 1)
    order = sort_phases(order, phases - 3, phases)
    keys_ref[:, :half] = order[:lines]
    keys_ref[:, half:] = order[lines:]
    outer(second, out_ref, 2)
    for side, present in sides:
        @pl.when(present)
        def _():
            tag_copy(side).wait_send()
            temp_copy(temp_hbm, 0, side).wait_send()
            temp_copy(first, 1, side).wait_send()
            temp_copy(second, 2, side).wait_send()


def split(x):
    high = x.astype(jnp.bfloat16)
    return high, (x - high.astype(jnp.float32)).astype(jnp.bfloat16)


def to_row(column):
    n = column.shape[0]
    return jnp.sum(jnp.where(iota((n, n), 0) == iota((n, n), 1), column, 0.0), axis=0, keepdims=True)


def to_column(row):
    n = row.shape[1]
    return jnp.sum(jnp.where(iota((n, n), 0) == iota((n, n), 1), row, 0.0), axis=1, keepdims=True)


def fields(key, lines, ny, nz):
    shift = log2(lines)
    col = (key >> shift) & (nz - 1)
    row = (key >> (shift + log2(nz))) & (ny - 1)
    return key & (lines - 1), col, row, key >> (shift + log2(nz) + log2(ny))


def hot_rows(plane, t, row, ny):
    hit = iota((ny, row.shape[1]), 0) == jnp.where(plane == t, row, -1)
    return jnp.where(hit, 1.0, 0.0).astype(jnp.bfloat16)


def find_starts(edge_ref, start_ref, shift):
    lines, wall = edge_ref.shape

    def clear(t, _):
        start_ref[t] = -1
        return 0

    lax.fori_loop(0, start_ref.shape[0], clear, 0)

    def block(b, _):
        def note(t, _):
            start_ref[t] = b
            return 0

        low = edge_ref[b, 0] >> shift
        return lax.fori_loop(low + 1, (edge_ref[b, wall - 1] >> shift) + 1, note, 0)

    lax.fori_loop(0, lines, block, 0)


def gather_kernel(
    heat_ref, keys_ref, surf_ref, ratio_ref, wall_ref, coef_ref, pieces, edge_ref, edge_sem, start_ref
):
    nx, ny, nz = heat_ref.shape
    lines, wall = keys_ref.shape
    plane_shift = log2(lines) + log2(nz) + log2(ny)
    load = pltpu.make_async_copy(keys_ref, edge_ref, edge_sem)
    load.start()

    def turn(plane, _):
        high, low = split(heat_ref[plane].T)
        pieces[plane, :nz] = high
        pieces[plane, nz:] = low
        return 0

    lax.fori_loop(0, nx, turn, 0)
    load.wait()
    find_starts(edge_ref, start_ref, plane_shift)

    def visit(b, t):
        line, col, row, plane = fields(keys_ref[pl.ds(b, 1), :], lines, ny, nz)
        hot = hot_rows(plane, t, row, ny)
        got = jnp.dot(pieces[jnp.maximum(t, 0)], hot, preferred_element_type=jnp.float32)
        at_col = iota((nz, wall), 0) == col
        return jnp.sum(jnp.where(at_col, got[:nz] + got[nz:], 0.0), axis=0, keepdims=True)

    def blocks(group, _):
        for i in range(GROUP):
            b = group * GROUP + i
            wall_ref[pl.ds(b, 1), :] = visit(b, edge_ref[b, 0] >> plane_shift)
        return 0

    lax.fori_loop(0, lines // GROUP, blocks, 0)

    places = [start_ref[t] for t in range(1, nx)]
    found = [visit(jnp.maximum(b, 0), jnp.where(b < 0, -2, t + 1)) for t, b in enumerate(places)]
    for b, temps in zip(places, found):
        rows = pl.ds(jnp.maximum(b, 0), 1)
        wall_ref[rows, :] = wall_ref[rows, :] + temps

    sums = jnp.zeros((lines, wall), jnp.float32)
    for b in range(lines):
        line = keys_ref[b : b + 1, :] & (lines - 1)
        sums = sums + jnp.where(iota((lines, wall), 0) == line, wall_ref[b : b + 1, :], 0.0)
    mean = to_row(jnp.sum(sums, axis=1, keepdims=True)) * (1.0 / wall)
    keep = jnp.exp(-ratio_ref[...] * surf_ref[...])
    coef_ref[...] = jnp.zeros(coef_ref.shape, jnp.float32)
    coef_ref[0:1, 0:lines] = keep
    coef_ref[1:2, 0:lines] = (1.0 - keep) * mean


def march_kernel(count, coef_ref, flag_ref, entry_ref, out_ref, every, send_sem, recv_sem):
    lines = flag_ref.shape[1]
    me = lax.axis_index("brick")
    pour = lax.axis_index("pour")

    def copy(offset, place):
        return pltpu.make_async_remote_copy(
            src_ref=coef_ref,
            dst_ref=every.at[place],
            send_sem=send_sem.at[offset],
            recv_sem=recv_sem.at[place],
            device_id=(pour, lax.rem(me + offset, count)),
            device_id_type=pl.DeviceIdType.MESH,
        )

    barrier = pltpu.get_barrier_semaphore()

    def greet(offset, _):
        pl.semaphore_signal(
            barrier, inc=1,
            device_id=(pour, lax.rem(me + offset, count)),
            device_id_type=pl.DeviceIdType.MESH,
        )
        return 0

    lax.fori_loop(1, count, greet, 0)
    pl.semaphore_wait(barrier, count - 1)

    def send(offset, _):
        copy(offset, me).start()
        return 0

    lax.fori_loop(1, count, send, 0)
    every[me] = coef_ref[...]

    def arrive(offset, _):
        copy(offset, lax.rem(me + offset, count)).wait_recv()
        return 0

    lax.fori_loop(1, count, arrive, 0)

    last = count - 1

    def flow(i, inflows):
        forward, backward = inflows
        up, down = every[i], every[last - i]
        forth = up[0:1, 0:lines] * forward + up[1:2, 0:lines]
        back = down[0:1, 0:lines] * backward + down[1:2, 0:lines]
        return jnp.where(i < me, forth, forward), jnp.where(last - i > me, back, backward)

    entry = entry_ref[...]
    forward, backward = lax.fori_loop(0, last, flow, (entry, entry), unroll=5)
    inflow = jnp.where(flag_ref[...] == 0, forward, backward)
    keep, gain = coef_ref[0:1, 0:lines], coef_ref[1:2, 0:lines]
    out_ref[...] = 0.5 * (inflow + keep * inflow + gain)

    def sent(offset, _):
        copy(offset, me).wait_send()
        return 0

    lax.fori_loop(1, count, sent, 0)


def scatter_kernel(
    heat_ref, keys_ref, wall_ref, coef_ref, cool_ref, out_ref, cool_out, edge_ref, edge_sem, start_ref
):
    nx, ny, nz = heat_ref.shape
    lines, wall = keys_ref.shape
    plane_shift = log2(lines) + log2(nz) + log2(ny)
    load = pltpu.make_async_copy(keys_ref, edge_ref, edge_sem)
    load.start()
    share = to_column(0.5 * (1.0 - coef_ref[0:1, 0:lines]))
    cool = to_column(cool_ref[...])
    cool_out[...] = cool_ref[...]

    def start(plane, _):
        out_ref[plane] = heat_ref[plane]
        return 0

    lax.fori_loop(0, nx, start, 0)
    load.wait()
    find_starts(edge_ref, start_ref, plane_shift)

    def visit(b, t):
        line, col, row, plane = fields(keys_ref[pl.ds(b, 1), :], lines, ny, nz)
        mine = iota((lines, wall), 0) == line
        share_row = jnp.sum(jnp.where(mine, share, 0.0), axis=0, keepdims=True)
        cool_row = jnp.sum(jnp.where(mine, cool, 0.0), axis=0, keepdims=True)
        high, low = split(share_row * (cool_row - wall_ref[pl.ds(b, 1), :]))
        at_col = iota((nz, wall), 0) == col
        parts = [
            jnp.where(at_col, part.astype(jnp.float32), 0.0).astype(jnp.bfloat16)
            for part in (high, low)
        ]
        hot = hot_rows(plane, t, row, ny)
        return lax.dot_general(
            jnp.concatenate([hot, hot], axis=1),
            jnp.concatenate(parts, axis=1),
            (((1,), (1,)), ((), ())),
            preferred_element_type=jnp.float32,
        )

    def blocks(group, _):
        places = [group * GROUP + i for i in range(GROUP)]
        planes = [edge_ref[b, 0] >> plane_shift for b in places]
        adds = [visit(b, t) for b, t in zip(places, planes)]
        for t, add in zip(planes, adds):
            out_ref[t] = out_ref[t] + add
        return 0

    lax.fori_loop(0, lines // GROUP, blocks, 0)

    places = [start_ref[t] for t in range(1, nx)]
    adds = [visit(jnp.maximum(b, 0), jnp.where(b < 0, -2, t + 1)) for t, b in enumerate(places)]
    for t, add in enumerate(adds):
        out_ref[t + 1] = out_ref[t + 1] + add


def per_device(count, temp, tags, cond_table, store_table, pos, surf, ratio, flag, entry):
    nx, ny, nz = temp.shape
    f32 = jnp.float32
    lines, wall = pos.shape[1:]
    pos, ratio, flag, entry = pos[0], ratio[None], flag[None], entry[None]
    local = pltpu.CompilerParams(vmem_limit_bytes=LIMIT)
    brick = (nx, ny, nz)
    heated, keys = pl.pallas_call(
        functools.partial(conduct_kernel, count),
        out_shape=(
            jax.ShapeDtypeStruct(brick, f32),
            jax.ShapeDtypeStruct((lines, wall), jnp.int32),
        ),
        in_specs=[HBM, HBM, HBM, HBM, HBM],
        out_specs=(VMEM, VMEM),
        scratch_shapes=[
            pltpu.VMEM((lines, wall), jnp.int32),
            pltpu.VMEM(brick, f32),
            pltpu.VMEM(brick, jnp.int32),
            pltpu.SMEM(cond_table.shape, f32),
            pltpu.SMEM(store_table.shape, f32),
            pltpu.VMEM(brick, f32),
            pltpu.VMEM(brick, f32),
            pltpu.VMEM(brick, f32),
            pltpu.VMEM(brick, f32),
            pltpu.VMEM((nx + 1, ny, nz), f32),
            pltpu.VMEM(brick, f32),
            pltpu.VMEM(brick, f32),
            pltpu.VMEM((STEPS, 2, ny, nz), f32),
            pltpu.VMEM((2, ny, nz), jnp.int32),
            pltpu.SemaphoreType.DMA((STEPS + 1, 2)),
            pltpu.SemaphoreType.DMA((STEPS + 1, 2)),
            pltpu.SemaphoreType.DMA((5,)),
        ],
        compiler_params=pltpu.CompilerParams(
            vmem_limit_bytes=LIMIT, collective_id=0, has_side_effects=True
        ),
        name="conduct",
    )(temp, tags, cond_table, store_table, pos)
    walls, coef = pl.pallas_call(
        gather_kernel,
        out_shape=(
            jax.ShapeDtypeStruct((lines, wall), f32),
            jax.ShapeDtypeStruct((2, 128), f32),
        ),
        in_specs=[VMEM, VMEM, VMEM, VMEM],
        out_specs=(VMEM, VMEM),
        scratch_shapes=[
            pltpu.VMEM((nx, 2 * nz, ny), jnp.bfloat16),
            pltpu.SMEM((lines, wall), jnp.int32),
            pltpu.SemaphoreType.DMA,
            pltpu.SMEM((nx,), jnp.int32),
        ],
        compiler_params=local,
        name="gather",
    )(heated, keys, surf, ratio)
    cool = pl.pallas_call(
        functools.partial(march_kernel, count),
        out_shape=jax.ShapeDtypeStruct((1, lines), f32),
        in_specs=[VMEM, VMEM, VMEM],
        out_specs=VMEM,
        scratch_shapes=[
            pltpu.VMEM((count, 2, 128), f32),
            pltpu.SemaphoreType.DMA((count,)),
            pltpu.SemaphoreType.DMA((count,)),
        ],
        compiler_params=pltpu.CompilerParams(
            vmem_limit_bytes=LIMIT, collective_id=1, has_side_effects=True
        ),
        name="march",
    )(coef, flag, entry)
    final, coolant = pl.pallas_call(
        scatter_kernel,
        out_shape=(
            jax.ShapeDtypeStruct(brick, f32),
            jax.ShapeDtypeStruct((1, lines), f32),
        ),
        in_specs=[VMEM, VMEM, VMEM, VMEM, VMEM],
        out_specs=(VMEM, VMEM),
        scratch_shapes=[
            pltpu.SMEM((lines, wall), jnp.int32),
            pltpu.SemaphoreType.DMA,
            pltpu.SMEM((nx,), jnp.int32),
        ],
        compiler_params=local,
        name="scatter",
    )(heated, keys, walls, coef, cool)
    return final, coolant


def solution(mesh):
    return jax.shard_map(
        functools.partial(per_device, mesh.shape["brick"]),
        mesh=mesh,
        in_specs=(
            P(("pour", "brick"), None, None),
            P("brick", None, None),
            P(),
            P(),
            P("brick", None, None),
            P("brick", None),
            P(),
            P(),
            P("pour"),
        ),
        out_specs=(P(("pour", "brick"), None, None), P(("pour", "brick"), None)),
        check_vma=False,
    )
```

```python
import functools

import jax
import jax.numpy as jnp
from jax import lax
from jax.experimental import pallas as pl
from jax.experimental.pallas import tpu as pltpu
from jax.sharding import PartitionSpec as P

STEPS = 3
ROWS = 32
PARTS = 2
GROUP = 8
VMEM = pl.BlockSpec(memory_space=pltpu.VMEM)
HBM = pl.BlockSpec(memory_space=pltpu.HBM)
LIMIT = 48 * 1024 * 1024


def log2(n):
    return n.bit_length() - 1


def iota(shape, dim):
    return lax.broadcasted_iota(jnp.int32, shape, dim)


def start_keys(pos_ref):
    lines, wall = pos_ref.shape
    half = wall // 2
    keys = pos_ref[...] * lines + iota((lines, wall), 0)
    return jnp.concatenate([keys[:, :half], keys[:, half:]], axis=0)


def sort_phases(x, first, last):
    half = x.shape[1]
    lines, wall = x.shape[0] // 2, 2 * half
    shape = x.shape
    row = iota(shape, 0)
    place = (row % lines) * wall + (row // lines) * half + iota(shape, 1)
    total = lines * wall
    for phase in range(first, last + 1):
        for stage in range(phase - 1, -1, -1):
            step = 1 << stage
            if step < half:
                axis, amount = 1, step
            elif step == half:
                axis, amount = 0, lines
            else:
                axis, amount = 0, step // wall
            size = shape[axis]
            low = (place & step) == 0
            up = pltpu.roll(x, size - amount, axis)
            down = up if 2 * amount == size else pltpu.roll(x, amount, axis)
            other = jnp.where(low, up, down)
            if phase == log2(total):
                take_min = low
            else:
                take_min = ((place >> stage) & 1) == ((place >> phase) & 1)
            x = jnp.where(take_min, jnp.minimum(x, other), jnp.maximum(x, other))
    return x


def pick(tags, table_ref):
    level = [table_ref[i] for i in range(table_ref.shape[0])]
    bit = 0
    while len(level) > 1:
        odd = (tags & (1 << bit)) != 0
        pairs = [level[i : i + 2] for i in range(0, len(level), 2)]
        level = [jnp.where(odd, p[1], p[0]) if len(p) == 2 else p[0] for p in pairs]
        bit += 1
    return level[0]


def inverse(x):
    guess = pl.reciprocal(x, approx=True)
    guess = guess * (2.0 - x * guess)
    return guess * (2.0 - x * guess)


def face_mean(left, right):
    return 2.0 * left * right * inverse(left + right + 1e-30)


def conduct_kernel(
    count,
    temp_hbm, tag_hbm, cond_hbm, store_hbm, pos_hbm, out_ref, keys_ref,
    pos_ref, temp_ref, tag_ref, cond_table, store_table,
    first, second, cond, coef, gx, gy, gz, temp_halo, tag_halo, send_sem, recv_sem, local_sem,
):
    nx, ny, nz = temp_ref.shape
    loads = [
        pltpu.make_async_copy(src, dst, local_sem.at[i])
        for i, (src, dst) in enumerate(
            [
                (tag_hbm, tag_ref),
                (cond_hbm, cond_table),
                (store_hbm, store_table),
                (temp_hbm, temp_ref),
                (pos_hbm, pos_ref),
            ]
        )
    ]
    for load in loads:
        load.start()
    me = lax.axis_index("brick")
    left, right = me - 1, me + 1
    has_left, has_right = me > 0, me < count - 1

    def copy(src, dst, slot, side, part):
        target = left if side == 0 else right
        return pltpu.make_async_remote_copy(
            src_ref=src,
            dst_ref=dst,
            send_sem=send_sem.at[slot, side, part],
            recv_sem=recv_sem.at[slot, 1 - side, part],
            device_id=(lax.axis_index("pour"), target),
            device_id_type=pl.DeviceIdType.MESH,
        )

    half_rows = ny // PARTS

    def tag_copy(side, part):
        rows = pl.ds(part * half_rows, half_rows)
        src = tag_hbm.at[0 if side == 0 else nx - 1, rows]
        return copy(src, tag_halo.at[1 - side, rows], STEPS, side, part)

    def temp_copy(src, step, side, part):
        rows = pl.ds(part * half_rows, half_rows)
        src = src.at[0 if side == 0 else nx - 1, rows]
        return copy(src, temp_halo.at[step, 1 - side, rows], step, side, part)

    sides = ((0, has_left), (1, has_right))
    barrier = pltpu.get_barrier_semaphore()
    for side, present in sides:
        @pl.when(present)
        def _():
            pl.semaphore_signal(
                barrier, inc=1,
                device_id=(lax.axis_index("pour"), left if side == 0 else right),
                device_id_type=pl.DeviceIdType.MESH,
            )
    pl.semaphore_wait(barrier, has_left.astype(jnp.int32) + has_right.astype(jnp.int32))
    for part in range(PARTS):
        for side, present in sides:
            @pl.when(present)
            def _():
                tag_copy(side, part).start()
                temp_copy(temp_hbm, 0, side, part).start()

    for side, present in sides:
        @pl.when(jnp.logical_not(present))
        def _():
            for step in range(STEPS):
                temp_halo[step, side] = jnp.zeros((ny, nz), jnp.float32)

    for load in loads:
        load.wait()

    chunks = [pl.ds(r, ROWS) for r in range(0, ny, ROWS)]
    row = iota((ROWS, nz), 0)
    lane = iota((ROWS, nz), 1)

    def below(ref, plane, r):
        if r + ROWS < ny:
            return ref[plane, pl.ds(r + 1, ROWS), :]
        here = ref[plane, pl.ds(r, ROWS), :]
        return jnp.where(row == ROWS - 1, here, pltpu.roll(here, ROWS - 1, 0))

    def properties(plane, _):
        for rows in chunks:
            tags = tag_ref[plane, rows, :]
            cond[plane, rows, :] = pick(tags, cond_table)
            coef[plane, rows, :] = 0.16 * inverse(pick(tags, store_table))
        return 0

    lax.fori_loop(0, nx, properties, 0)

    def faces(plane, _):
        for r, rows in zip(range(0, ny, ROWS), chunks):
            here = cond[plane, rows, :]
            gy[plane, rows, :] = face_mean(here, below(cond, plane, r))
            side = face_mean(here, pltpu.roll(here, nz - 1, 1))
            gz[plane, rows, :] = jnp.where(lane == nz - 1, 0.0, side)
        return 0

    lax.fori_loop(0, nx, faces, 0)

    def faces_x(plane, _):
        for rows in chunks:
            gx[plane, rows, :] = face_mean(cond[plane - 1, rows, :], cond[plane, rows, :])
        return 0

    lax.fori_loop(1, nx, faces_x, 0)

    def update(src, dst, plane, before, after, begin=0, end=ny):
        last = jnp.zeros((8, nz), jnp.float32)
        if begin:
            near = pl.ds(begin - 8, 8)
            change = src[plane, pl.ds(begin - 7, 8), :] - src[plane, near, :]
            last = pltpu.roll(gy[plane, near, :] * change, 1, 0)
        for r in range(begin, end, ROWS):
            rows = pl.ds(r, ROWS)
            here = src[plane, rows, :]
            flux = gx[plane + 1, rows, :] * (after(rows) - here)
            flux = flux - gx[plane, rows, :] * (here - before(rows))
            side = gy[plane, rows, :] * (below(src, plane, r) - here)
            turned = pltpu.roll(side, 1, 0)
            top = jnp.where(row[:8] == 0, last, turned[:8])
            last = turned[:8]
            flux = flux + (side - jnp.concatenate([top, turned[8:]], axis=0))
            side = gz[plane, rows, :] * (pltpu.roll(here, nz - 1, 1) - here)
            flux = flux + (side - pltpu.roll(side, 1, 1))
            dst[plane, rows, :] = here + coef[plane, rows, :] * flux

    def inner(src, dst, first_plane, last_plane):
        def body(plane, _):
            update(
                src, dst, plane,
                lambda rows: src[plane - 1, rows, :],
                lambda rows: src[plane + 1, rows, :],
            )
            return 0

        lax.fori_loop(first_plane, last_plane + 1, body, 0)

    def pair(src, dst, plane):
        inner(src, dst, plane, plane)
        inner(src, dst, nx - 1 - plane, nx - 1 - plane)

    def outer(src, dst, step, part):
        begin, end = part * half_rows, (part + 1) * half_rows
        for side, present in sides:
            edge, inside, face = (0, 1, 0) if side == 0 else (nx - 1, nx - 2, nx)

            @pl.when(present)
            def _():
                temp_copy(src, step, 1 - side, part).wait_recv()

            if step == 0:
                @pl.when(present)
                def _():
                    tag_copy(1 - side, part).wait_recv()
                    for r in range(begin, end, ROWS):
                        rows = pl.ds(r, ROWS)
                        beyond = pick(tag_halo[side, rows, :], cond_table)
                        gx[face, rows, :] = face_mean(beyond, cond[edge, rows, :])

                @pl.when(jnp.logical_not(present))
                def _():
                    gx[face, begin:end, :] = jnp.zeros((half_rows, nz), jnp.float32)

            def halo(rows):
                return temp_halo[step, side, rows, :]

            def inward(rows):
                return src[inside, rows, :]

            before, after = (halo, inward) if side == 0 else (inward, halo)
            update(src, dst, edge, before, after, begin, end)
            if step + 1 < STEPS:
                @pl.when(present)
                def _():
                    temp_copy(dst, step + 1, side, part).start()

    lines, wall = pos_ref.shape
    half = wall // 2
    phases = log2(lines * wall)
    inner(temp_ref, first, 1, nx - 2)
    outer(temp_ref, first, 0, 0)
    inner(first, second, 2, nx - 3)
    inner(second, out_ref, 3, nx - 4)
    outer(temp_ref, first, 0, 1)
    pair(first, second, 1)
    pair(second, out_ref, 2)
    outer(first, second, 1, 0)
    order = sort_phases(start_keys(pos_ref), 1, phases - 4)
    outer(first, second, 1, 1)
    pair(second, out_ref, 1)
    order = sort_phases(order, phases - 3, phases)
    keys_ref[:, :half] = order[:lines]
    keys_ref[:, half:] = order[lines:]
    outer(second, out_ref, 2, 0)
    outer(second, out_ref, 2, 1)
    for part in range(PARTS):
        for side, present in sides:
            @pl.when(present)
            def _():
                tag_copy(side, part).wait_send()
                temp_copy(temp_hbm, 0, side, part).wait_send()
                temp_copy(first, 1, side, part).wait_send()
                temp_copy(second, 2, side, part).wait_send()


def split(x):
    high = x.astype(jnp.bfloat16)
    return high, (x - high.astype(jnp.float32)).astype(jnp.bfloat16)


def to_row(column):
    n = column.shape[0]
    return jnp.sum(jnp.where(iota((n, n), 0) == iota((n, n), 1), column, 0.0), axis=0, keepdims=True)


def to_column(row):
    n = row.shape[1]
    return jnp.sum(jnp.where(iota((n, n), 0) == iota((n, n), 1), row, 0.0), axis=1, keepdims=True)


def fields(key, lines, ny, nz):
    shift = log2(lines)
    col = (key >> shift) & (nz - 1)
    row = (key >> (shift + log2(nz))) & (ny - 1)
    return key & (lines - 1), col, row, key >> (shift + log2(nz) + log2(ny))


def hot_rows(plane, t, row, ny):
    hit = iota((ny, row.shape[1]), 0) == jnp.where(plane == t, row, -1)
    return jnp.where(hit, 1.0, 0.0).astype(jnp.bfloat16)


def find_starts(edge_ref, start_ref, shift):
    lines, wall = edge_ref.shape

    def clear(t, _):
        start_ref[t] = -1
        return 0

    lax.fori_loop(0, start_ref.shape[0], clear, 0)

    def block(b, _):
        def note(t, _):
            start_ref[t] = b
            return 0

        low = edge_ref[b, 0] >> shift
        return lax.fori_loop(low + 1, (edge_ref[b, wall - 1] >> shift) + 1, note, 0)

    lax.fori_loop(0, lines, block, 0)


def gather_kernel(
    heat_ref, keys_ref, surf_ref, ratio_ref, wall_ref, coef_ref, pieces, edge_ref, edge_sem, start_ref
):
    nx, ny, nz = heat_ref.shape
    lines, wall = keys_ref.shape
    plane_shift = log2(lines) + log2(nz) + log2(ny)
    load = pltpu.make_async_copy(keys_ref, edge_ref, edge_sem)
    load.start()

    def turn(plane, _):
        high, low = split(heat_ref[plane].T)
        pieces[plane, :nz] = high
        pieces[plane, nz:] = low
        return 0

    lax.fori_loop(0, nx, turn, 0)
    load.wait()
    find_starts(edge_ref, start_ref, plane_shift)

    def visit(b, t):
        line, col, row, plane = fields(keys_ref[pl.ds(b, 1), :], lines, ny, nz)
        hot = hot_rows(plane, t, row, ny)
        got = jnp.dot(pieces[jnp.maximum(t, 0)], hot, preferred_element_type=jnp.float32)
        at_col = iota((nz, wall), 0) == col
        return jnp.sum(jnp.where(at_col, got[:nz] + got[nz:], 0.0), axis=0, keepdims=True)

    def blocks(group, _):
        for i in range(GROUP):
            b = group * GROUP + i
            wall_ref[pl.ds(b, 1), :] = visit(b, edge_ref[b, 0] >> plane_shift)
        return 0

    lax.fori_loop(0, lines // GROUP, blocks, 0)

    places = [start_ref[t] for t in range(1, nx)]
    found = [visit(jnp.maximum(b, 0), jnp.where(b < 0, -2, t + 1)) for t, b in enumerate(places)]
    for b, temps in zip(places, found):
        rows = pl.ds(jnp.maximum(b, 0), 1)
        wall_ref[rows, :] = wall_ref[rows, :] + temps

    sums = jnp.zeros((lines, wall), jnp.float32)
    for b in range(lines):
        line = keys_ref[b : b + 1, :] & (lines - 1)
        sums = sums + jnp.where(iota((lines, wall), 0) == line, wall_ref[b : b + 1, :], 0.0)
    mean = to_row(jnp.sum(sums, axis=1, keepdims=True)) * (1.0 / wall)
    keep = jnp.exp(-ratio_ref[...] * surf_ref[...])
    coef_ref[...] = jnp.zeros(coef_ref.shape, jnp.float32)
    coef_ref[0:1, 0:lines] = keep
    coef_ref[1:2, 0:lines] = (1.0 - keep) * mean


def march_kernel(count, coef_ref, flag_ref, entry_ref, out_ref, every, send_sem, recv_sem):
    lines = flag_ref.shape[1]
    me = lax.axis_index("brick")
    pour = lax.axis_index("pour")

    def copy(offset, place):
        return pltpu.make_async_remote_copy(
            src_ref=coef_ref,
            dst_ref=every.at[place],
            send_sem=send_sem.at[offset],
            recv_sem=recv_sem.at[place],
            device_id=(pour, lax.rem(me + offset, count)),
            device_id_type=pl.DeviceIdType.MESH,
        )

    barrier = pltpu.get_barrier_semaphore()

    def greet(offset, _):
        pl.semaphore_signal(
            barrier, inc=1,
            device_id=(pour, lax.rem(me + offset, count)),
            device_id_type=pl.DeviceIdType.MESH,
        )
        return 0

    lax.fori_loop(1, count, greet, 0)
    pl.semaphore_wait(barrier, count - 1)

    def send(offset, _):
        copy(offset, me).start()
        return 0

    lax.fori_loop(1, count, send, 0)
    every[me] = coef_ref[...]

    def arrive(offset, _):
        copy(offset, lax.rem(me + offset, count)).wait_recv()
        return 0

    lax.fori_loop(1, count, arrive, 0)

    last = count - 1

    def flow(i, inflows):
        forward, backward = inflows
        up, down = every[i], every[last - i]
        forth = up[0:1, 0:lines] * forward + up[1:2, 0:lines]
        back = down[0:1, 0:lines] * backward + down[1:2, 0:lines]
        return jnp.where(i < me, forth, forward), jnp.where(last - i > me, back, backward)

    entry = entry_ref[...]
    forward, backward = lax.fori_loop(0, last, flow, (entry, entry), unroll=5)
    inflow = jnp.where(flag_ref[...] == 0, forward, backward)
    keep, gain = coef_ref[0:1, 0:lines], coef_ref[1:2, 0:lines]
    out_ref[...] = 0.5 * (inflow + keep * inflow + gain)

    def sent(offset, _):
        copy(offset, me).wait_send()
        return 0

    lax.fori_loop(1, count, sent, 0)


def scatter_kernel(
    heat_ref, keys_ref, wall_ref, coef_ref, cool_ref, out_ref, cool_out, edge_ref, edge_sem, start_ref
):
    nx, ny, nz = heat_ref.shape
    lines, wall = keys_ref.shape
    plane_shift = log2(lines) + log2(nz) + log2(ny)
    load = pltpu.make_async_copy(keys_ref, edge_ref, edge_sem)
    load.start()
    share = to_column(0.5 * (1.0 - coef_ref[0:1, 0:lines]))
    cool = to_column(cool_ref[...])
    cool_out[...] = cool_ref[...]

    def start(plane, _):
        out_ref[plane] = heat_ref[plane]
        return 0

    lax.fori_loop(0, nx, start, 0)
    load.wait()
    find_starts(edge_ref, start_ref, plane_shift)

    def visit(b, t):
        line, col, row, plane = fields(keys_ref[pl.ds(b, 1), :], lines, ny, nz)
        mine = iota((lines, wall), 0) == line
        share_row = jnp.sum(jnp.where(mine, share, 0.0), axis=0, keepdims=True)
        cool_row = jnp.sum(jnp.where(mine, cool, 0.0), axis=0, keepdims=True)
        high, low = split(share_row * (cool_row - wall_ref[pl.ds(b, 1), :]))
        at_col = iota((nz, wall), 0) == col
        parts = [
            jnp.where(at_col, part.astype(jnp.float32), 0.0).astype(jnp.bfloat16)
            for part in (high, low)
        ]
        hot = hot_rows(plane, t, row, ny)
        return lax.dot_general(
            jnp.concatenate([hot, hot], axis=1),
            jnp.concatenate(parts, axis=1),
            (((1,), (1,)), ((), ())),
            preferred_element_type=jnp.float32,
        )

    def blocks(group, _):
        places = [group * GROUP + i for i in range(GROUP)]
        planes = [edge_ref[b, 0] >> plane_shift for b in places]
        adds = [visit(b, t) for b, t in zip(places, planes)]
        for t, add in zip(planes, adds):
            out_ref[t] = out_ref[t] + add
        return 0

    lax.fori_loop(0, lines // GROUP, blocks, 0)

    places = [start_ref[t] for t in range(1, nx)]
    adds = [visit(jnp.maximum(b, 0), jnp.where(b < 0, -2, t + 1)) for t, b in enumerate(places)]
    for t, add in enumerate(adds):
        out_ref[t + 1] = out_ref[t + 1] + add


def per_device(count, temp, tags, cond_table, store_table, pos, surf, ratio, flag, entry):
    nx, ny, nz = temp.shape
    f32 = jnp.float32
    lines, wall = pos.shape[1:]
    pos, ratio, flag, entry = pos[0], ratio[None], flag[None], entry[None]
    local = pltpu.CompilerParams(vmem_limit_bytes=LIMIT)
    brick = (nx, ny, nz)
    heated, keys = pl.pallas_call(
        functools.partial(conduct_kernel, count),
        out_shape=(
            jax.ShapeDtypeStruct(brick, f32),
            jax.ShapeDtypeStruct((lines, wall), jnp.int32),
        ),
        in_specs=[HBM, HBM, HBM, HBM, HBM],
        out_specs=(VMEM, VMEM),
        scratch_shapes=[
            pltpu.VMEM((lines, wall), jnp.int32),
            pltpu.VMEM(brick, f32),
            pltpu.VMEM(brick, jnp.int32),
            pltpu.SMEM(cond_table.shape, f32),
            pltpu.SMEM(store_table.shape, f32),
            pltpu.VMEM(brick, f32),
            pltpu.VMEM(brick, f32),
            pltpu.VMEM(brick, f32),
            pltpu.VMEM(brick, f32),
            pltpu.VMEM((nx + 1, ny, nz), f32),
            pltpu.VMEM(brick, f32),
            pltpu.VMEM(brick, f32),
            pltpu.VMEM((STEPS, 2, ny, nz), f32),
            pltpu.VMEM((2, ny, nz), jnp.int32),
            pltpu.SemaphoreType.DMA((STEPS + 1, 2, PARTS)),
            pltpu.SemaphoreType.DMA((STEPS + 1, 2, PARTS)),
            pltpu.SemaphoreType.DMA((5,)),
        ],
        compiler_params=pltpu.CompilerParams(
            vmem_limit_bytes=62 * 1024 * 1024, collective_id=0, has_side_effects=True
        ),
        name="conduct",
    )(temp, tags, cond_table, store_table, pos)
    walls, coef = pl.pallas_call(
        gather_kernel,
        out_shape=(
            jax.ShapeDtypeStruct((lines, wall), f32),
            jax.ShapeDtypeStruct((2, 128), f32),
        ),
        in_specs=[VMEM, VMEM, VMEM, VMEM],
        out_specs=(VMEM, VMEM),
        scratch_shapes=[
            pltpu.VMEM((nx, 2 * nz, ny), jnp.bfloat16),
            pltpu.SMEM((lines, wall), jnp.int32),
            pltpu.SemaphoreType.DMA,
            pltpu.SMEM((nx,), jnp.int32),
        ],
        compiler_params=local,
        name="gather",
    )(heated, keys, surf, ratio)
    cool = pl.pallas_call(
        functools.partial(march_kernel, count),
        out_shape=jax.ShapeDtypeStruct((1, lines), f32),
        in_specs=[VMEM, VMEM, VMEM],
        out_specs=VMEM,
        scratch_shapes=[
            pltpu.VMEM((count, 2, 128), f32),
            pltpu.SemaphoreType.DMA((count,)),
            pltpu.SemaphoreType.DMA((count,)),
        ],
        compiler_params=pltpu.CompilerParams(
            vmem_limit_bytes=LIMIT, collective_id=1, has_side_effects=True
        ),
        name="march",
    )(coef, flag, entry)
    final, coolant = pl.pallas_call(
        scatter_kernel,
        out_shape=(
            jax.ShapeDtypeStruct(brick, f32),
            jax.ShapeDtypeStruct((1, lines), f32),
        ),
        in_specs=[VMEM, VMEM, VMEM, VMEM, VMEM],
        out_specs=(VMEM, VMEM),
        scratch_shapes=[
            pltpu.SMEM((lines, wall), jnp.int32),
            pltpu.SemaphoreType.DMA,
            pltpu.SMEM((nx,), jnp.int32),
        ],
        compiler_params=local,
        name="scatter",
    )(heated, keys, walls, coef, cool)
    return final, coolant


def solution(mesh):
    return jax.shard_map(
        functools.partial(per_device, mesh.shape["brick"]),
        mesh=mesh,
        in_specs=(
            P(("pour", "brick"), None, None),
            P("brick", None, None),
            P(),
            P(),
            P("brick", None, None),
            P("brick", None),
            P(),
            P(),
            P("pour"),
        ),
        out_specs=(P(("pour", "brick"), None, None), P(("pour", "brick"), None)),
        check_vma=False,
    )
```

```python
import functools

import jax
import jax.numpy as jnp
from jax import lax
from jax.experimental import pallas as pl
from jax.experimental.pallas import tpu as pltpu
from jax.sharding import PartitionSpec as P

STEPS = 3
ROWS = 32
PARTS = 2
GROUP = 8
VMEM = pl.BlockSpec(memory_space=pltpu.VMEM)
HBM = pl.BlockSpec(memory_space=pltpu.HBM)
LIMIT = 62 * 1024 * 1024


def log2(n):
    return n.bit_length() - 1


def iota(shape, dim):
    return lax.broadcasted_iota(jnp.int32, shape, dim)


def start_keys(pos_ref):
    lines, wall = pos_ref.shape
    half = wall // 2
    keys = pos_ref[...] * lines + iota((lines, wall), 0)
    return jnp.concatenate([keys[:, :half], keys[:, half:]], axis=0)


def sort_phases(x, first, last):
    half = x.shape[1]
    lines, wall = x.shape[0] // 2, 2 * half
    shape = x.shape
    row = iota(shape, 0)
    place = (row % lines) * wall + (row // lines) * half + iota(shape, 1)
    total = lines * wall
    for phase in range(first, last + 1):
        for stage in range(phase - 1, -1, -1):
            step = 1 << stage
            if step < half:
                axis, amount = 1, step
            elif step == half:
                axis, amount = 0, lines
            else:
                axis, amount = 0, step // wall
            size = shape[axis]
            low = (place & step) == 0
            up = pltpu.roll(x, size - amount, axis)
            down = up if 2 * amount == size else pltpu.roll(x, amount, axis)
            other = jnp.where(low, up, down)
            if phase == log2(total):
                take_min = low
            else:
                take_min = ((place >> stage) & 1) == ((place >> phase) & 1)
            x = jnp.where(take_min, jnp.minimum(x, other), jnp.maximum(x, other))
    return x


def pick(tags, table_ref):
    level = [table_ref[i] for i in range(table_ref.shape[0])]
    bit = 0
    while len(level) > 1:
        odd = (tags & (1 << bit)) != 0
        pairs = [level[i : i + 2] for i in range(0, len(level), 2)]
        level = [jnp.where(odd, p[1], p[0]) if len(p) == 2 else p[0] for p in pairs]
        bit += 1
    return level[0]


def inverse(x):
    guess = pl.reciprocal(x, approx=True)
    guess = guess * (2.0 - x * guess)
    return guess * (2.0 - x * guess)


def face_mean(left, right):
    return 2.0 * left * right * inverse(left + right + 1e-30)


def conduct_kernel(
    count,
    temp_hbm, tag_hbm, cond_hbm, store_hbm, pos_hbm, out_hbm, keys_ref,
    out_ref, out_sem, pos_ref, temp_ref, tag_ref, cond_table, store_table,
    first, second, cond, coef, gx, gy, gz, temp_halo, tag_halo, send_sem, recv_sem, local_sem,
):
    nx, ny, nz = temp_ref.shape
    loads = [
        pltpu.make_async_copy(src, dst, local_sem.at[i])
        for i, (src, dst) in enumerate(
            [
                (tag_hbm, tag_ref),
                (cond_hbm, cond_table),
                (store_hbm, store_table),
                (temp_hbm, temp_ref),
                (pos_hbm, pos_ref),
            ]
        )
    ]
    for load in loads:
        load.start()
    me = lax.axis_index("brick")
    left, right = me - 1, me + 1
    has_left, has_right = me > 0, me < count - 1

    def copy(src, dst, slot, side, part):
        target = left if side == 0 else right
        return pltpu.make_async_remote_copy(
            src_ref=src,
            dst_ref=dst,
            send_sem=send_sem.at[slot, side, part],
            recv_sem=recv_sem.at[slot, 1 - side, part],
            device_id=(lax.axis_index("pour"), target),
            device_id_type=pl.DeviceIdType.MESH,
        )

    half_rows = ny // PARTS

    def tag_copy(side, part):
        rows = pl.ds(part * half_rows, half_rows)
        src = tag_hbm.at[0 if side == 0 else nx - 1, rows]
        return copy(src, tag_halo.at[1 - side, rows], STEPS, side, part)

    def temp_copy(src, step, side, part):
        rows = pl.ds(part * half_rows, half_rows)
        src = src.at[0 if side == 0 else nx - 1, rows]
        return copy(src, temp_halo.at[step, 1 - side, rows], step, side, part)

    sides = ((0, has_left), (1, has_right))
    barrier = pltpu.get_barrier_semaphore()
    for side, present in sides:
        @pl.when(present)
        def _():
            pl.semaphore_signal(
                barrier, inc=1,
                device_id=(lax.axis_index("pour"), left if side == 0 else right),
                device_id_type=pl.DeviceIdType.MESH,
            )
    pl.semaphore_wait(barrier, has_left.astype(jnp.int32) + has_right.astype(jnp.int32))
    for part in range(PARTS):
        for side, present in sides:
            @pl.when(present)
            def _():
                tag_copy(side, part).start()
                temp_copy(temp_hbm, 0, side, part).start()

    for side, present in sides:
        @pl.when(jnp.logical_not(present))
        def _():
            for step in range(STEPS):
                temp_halo[step, side] = jnp.zeros((ny, nz), jnp.float32)

    for load in loads:
        load.wait()

    chunks = [pl.ds(r, ROWS) for r in range(0, ny, ROWS)]
    row = iota((ROWS, nz), 0)
    lane = iota((ROWS, nz), 1)

    def below(ref, plane, r):
        if r + ROWS < ny:
            return ref[plane, pl.ds(r + 1, ROWS), :]
        here = ref[plane, pl.ds(r, ROWS), :]
        return jnp.where(row == ROWS - 1, here, pltpu.roll(here, ROWS - 1, 0))

    def properties(plane, _):
        for rows in chunks:
            tags = tag_ref[plane, rows, :]
            cond[plane, rows, :] = pick(tags, cond_table)
            coef[plane, rows, :] = 0.16 * inverse(pick(tags, store_table))
        return 0

    lax.fori_loop(0, nx, properties, 0)

    def faces(plane, _):
        for r, rows in zip(range(0, ny, ROWS), chunks):
            here = cond[plane, rows, :]
            gy[plane, rows, :] = face_mean(here, below(cond, plane, r))
            side = face_mean(here, pltpu.roll(here, nz - 1, 1))
            gz[plane, rows, :] = jnp.where(lane == nz - 1, 0.0, side)
        return 0

    lax.fori_loop(0, nx, faces, 0)

    def faces_x(plane, _):
        for rows in chunks:
            gx[plane, rows, :] = face_mean(cond[plane - 1, rows, :], cond[plane, rows, :])
        return 0

    lax.fori_loop(1, nx, faces_x, 0)

    def update(src, dst, plane, before, after, begin=0, end=ny):
        last = jnp.zeros((8, nz), jnp.float32)
        if begin:
            near = pl.ds(begin - 8, 8)
            change = src[plane, pl.ds(begin - 7, 8), :] - src[plane, near, :]
            last = pltpu.roll(gy[plane, near, :] * change, 1, 0)
        for r in range(begin, end, ROWS):
            rows = pl.ds(r, ROWS)
            here = src[plane, rows, :]
            flux = gx[plane + 1, rows, :] * (after(rows) - here)
            flux = flux - gx[plane, rows, :] * (here - before(rows))
            side = gy[plane, rows, :] * (below(src, plane, r) - here)
            turned = pltpu.roll(side, 1, 0)
            top = jnp.where(row[:8] == 0, last, turned[:8])
            last = turned[:8]
            flux = flux + (side - jnp.concatenate([top, turned[8:]], axis=0))
            side = gz[plane, rows, :] * (pltpu.roll(here, nz - 1, 1) - here)
            flux = flux + (side - pltpu.roll(side, 1, 1))
            dst[plane, rows, :] = here + coef[plane, rows, :] * flux

    def inner(src, dst, first_plane, last_plane):
        def body(plane, _):
            update(
                src, dst, plane,
                lambda rows: src[plane - 1, rows, :],
                lambda rows: src[plane + 1, rows, :],
            )
            return 0

        lax.fori_loop(first_plane, last_plane + 1, body, 0)

    def pair(src, dst, plane):
        inner(src, dst, plane, plane)
        inner(src, dst, nx - 1 - plane, nx - 1 - plane)

    def outer(src, dst, step, part):
        begin, end = part * half_rows, (part + 1) * half_rows
        for side, present in sides:
            edge, inside, face = (0, 1, 0) if side == 0 else (nx - 1, nx - 2, nx)

            @pl.when(present)
            def _():
                temp_copy(src, step, 1 - side, part).wait_recv()

            if step == 0:
                @pl.when(present)
                def _():
                    tag_copy(1 - side, part).wait_recv()
                    for r in range(begin, end, ROWS):
                        rows = pl.ds(r, ROWS)
                        beyond = pick(tag_halo[side, rows, :], cond_table)
                        gx[face, rows, :] = face_mean(beyond, cond[edge, rows, :])

                @pl.when(jnp.logical_not(present))
                def _():
                    gx[face, begin:end, :] = jnp.zeros((half_rows, nz), jnp.float32)

            def halo(rows):
                return temp_halo[step, side, rows, :]

            def inward(rows):
                return src[inside, rows, :]

            before, after = (halo, inward) if side == 0 else (inward, halo)
            update(src, dst, edge, before, after, begin, end)
            if step + 1 < STEPS:
                @pl.when(present)
                def _():
                    temp_copy(dst, step + 1, side, part).start()

    def hand_out(*planes):
        return [
            pltpu.make_async_copy(out_ref.at[i], out_hbm.at[i], out_sem.at[i]) for i in planes
        ]

    lines, wall = pos_ref.shape
    half = wall // 2
    phases = log2(lines * wall)
    inner(temp_ref, first, 1, nx - 2)
    outer(temp_ref, first, 0, 0)
    inner(first, second, 2, nx - 3)
    inner(second, out_ref, 3, nx - 4)
    for store in hand_out(*range(3, nx - 3)):
        store.start()
    outer(temp_ref, first, 0, 1)
    pair(first, second, 1)
    pair(second, out_ref, 2)
    for store in hand_out(2, nx - 3):
        store.start()
    outer(first, second, 1, 0)
    order = sort_phases(start_keys(pos_ref), 1, phases - 4)
    outer(first, second, 1, 1)
    pair(second, out_ref, 1)
    for store in hand_out(1, nx - 2):
        store.start()
    order = sort_phases(order, phases - 3, phases)
    keys_ref[:, :half] = order[:lines]
    keys_ref[:, half:] = order[lines:]
    outer(second, out_ref, 2, 0)
    outer(second, out_ref, 2, 1)
    for store in hand_out(0, nx - 1):
        store.start()
    for store in hand_out(*range(nx)):
        store.wait()
    for part in range(PARTS):
        for side, present in sides:
            @pl.when(present)
            def _():
                tag_copy(side, part).wait_send()
                temp_copy(temp_hbm, 0, side, part).wait_send()
                temp_copy(first, 1, side, part).wait_send()
                temp_copy(second, 2, side, part).wait_send()


def split(x):
    high = x.astype(jnp.bfloat16)
    return high, (x - high.astype(jnp.float32)).astype(jnp.bfloat16)


def to_row(column):
    n = column.shape[0]
    return jnp.sum(jnp.where(iota((n, n), 0) == iota((n, n), 1), column, 0.0), axis=0, keepdims=True)


def to_column(row):
    n = row.shape[1]
    return jnp.sum(jnp.where(iota((n, n), 0) == iota((n, n), 1), row, 0.0), axis=1, keepdims=True)


def fields(key, lines, ny, nz):
    shift = log2(lines)
    col = (key >> shift) & (nz - 1)
    row = (key >> (shift + log2(nz))) & (ny - 1)
    return key & (lines - 1), col, row, key >> (shift + log2(nz) + log2(ny))


def hot_rows(plane, t, row, ny):
    hit = iota((ny, row.shape[1]), 0) == jnp.where(plane == t, row, -1)
    return jnp.where(hit, 1.0, 0.0).astype(jnp.bfloat16)


def find_starts(edge_ref, start_ref, shift):
    lines, wall = edge_ref.shape

    def clear(t, _):
        start_ref[t] = -1
        return 0

    lax.fori_loop(0, start_ref.shape[0], clear, 0)

    def block(b, _):
        def note(t, _):
            start_ref[t] = b
            return 0

        low = edge_ref[b, 0] >> shift
        return lax.fori_loop(low + 1, (edge_ref[b, wall - 1] >> shift) + 1, note, 0)

    lax.fori_loop(0, lines, block, 0)


def gather_kernel(
    heat_hbm, keys_hbm, surf_ref, ratio_ref, wall_ref, coef_ref,
    heat_ref, heat_sem, keys_ref, keys_sem, pieces, edge_ref, edge_sem, start_ref
):
    nx, ny, nz = heat_hbm.shape
    lines, wall = keys_hbm.shape
    for plane in range(nx):
        pltpu.make_async_copy(heat_hbm.at[plane], heat_ref.at[plane], heat_sem.at[plane]).start()
    keys_load = pltpu.make_async_copy(keys_hbm, keys_ref, keys_sem)
    keys_load.start()
    plane_shift = log2(lines) + log2(nz) + log2(ny)
    load = pltpu.make_async_copy(keys_hbm, edge_ref, edge_sem)
    load.start()

    def turn(plane, _):
        pltpu.make_async_copy(
            heat_hbm.at[plane], heat_ref.at[plane], heat_sem.at[plane]
        ).wait()
        high, low = split(heat_ref[plane].T)
        pieces[plane, :nz] = high
        pieces[plane, nz:] = low
        return 0

    lax.fori_loop(0, nx, turn, 0)
    load.wait()
    keys_load.wait()
    find_starts(edge_ref, start_ref, plane_shift)

    def visit(b, t):
        line, col, row, plane = fields(keys_ref[pl.ds(b, 1), :], lines, ny, nz)
        hot = hot_rows(plane, t, row, ny)
        got = jnp.dot(pieces[jnp.maximum(t, 0)], hot, preferred_element_type=jnp.float32)
        at_col = iota((nz, wall), 0) == col
        return jnp.sum(jnp.where(at_col, got[:nz] + got[nz:], 0.0), axis=0, keepdims=True)

    def blocks(group, _):
        for i in range(GROUP):
            b = group * GROUP + i
            wall_ref[pl.ds(b, 1), :] = visit(b, edge_ref[b, 0] >> plane_shift)
        return 0

    lax.fori_loop(0, lines // GROUP, blocks, 0)

    places = [start_ref[t] for t in range(1, nx)]
    found = [visit(jnp.maximum(b, 0), jnp.where(b < 0, -2, t + 1)) for t, b in enumerate(places)]
    for b, temps in zip(places, found):
        rows = pl.ds(jnp.maximum(b, 0), 1)
        wall_ref[rows, :] = wall_ref[rows, :] + temps

    sums = jnp.zeros((lines, wall), jnp.float32)
    for b in range(lines):
        line = keys_ref[b : b + 1, :] & (lines - 1)
        sums = sums + jnp.where(iota((lines, wall), 0) == line, wall_ref[b : b + 1, :], 0.0)
    mean = to_row(jnp.sum(sums, axis=1, keepdims=True)) * (1.0 / wall)
    keep = jnp.exp(-ratio_ref[...] * surf_ref[...])
    coef_ref[...] = jnp.zeros(coef_ref.shape, jnp.float32)
    coef_ref[0:1, 0:lines] = keep
    coef_ref[1:2, 0:lines] = (1.0 - keep) * mean


def march_kernel(count, coef_ref, flag_ref, entry_ref, out_ref, every, send_sem, recv_sem):
    lines = flag_ref.shape[1]
    me = lax.axis_index("brick")
    pour = lax.axis_index("pour")

    def copy(offset, place):
        return pltpu.make_async_remote_copy(
            src_ref=coef_ref,
            dst_ref=every.at[place],
            send_sem=send_sem.at[offset],
            recv_sem=recv_sem.at[place],
            device_id=(pour, lax.rem(me + offset, count)),
            device_id_type=pl.DeviceIdType.MESH,
        )

    barrier = pltpu.get_barrier_semaphore()

    def greet(offset, _):
        pl.semaphore_signal(
            barrier, inc=1,
            device_id=(pour, lax.rem(me + offset, count)),
            device_id_type=pl.DeviceIdType.MESH,
        )
        return 0

    lax.fori_loop(1, count, greet, 0)
    pl.semaphore_wait(barrier, count - 1)

    def send(offset, _):
        copy(offset, me).start()
        return 0

    lax.fori_loop(1, count, send, 0)
    every[me] = coef_ref[...]

    def arrive(offset, _):
        copy(offset, lax.rem(me + offset, count)).wait_recv()
        return 0

    lax.fori_loop(1, count, arrive, 0)

    last = count - 1

    def flow(i, inflows):
        forward, backward = inflows
        up, down = every[i], every[last - i]
        forth = up[0:1, 0:lines] * forward + up[1:2, 0:lines]
        back = down[0:1, 0:lines] * backward + down[1:2, 0:lines]
        return jnp.where(i < me, forth, forward), jnp.where(last - i > me, back, backward)

    entry = entry_ref[...]
    forward, backward = lax.fori_loop(0, last, flow, (entry, entry), unroll=5)
    inflow = jnp.where(flag_ref[...] == 0, forward, backward)
    keep, gain = coef_ref[0:1, 0:lines], coef_ref[1:2, 0:lines]
    out_ref[...] = 0.5 * (inflow + keep * inflow + gain)

    def sent(offset, _):
        copy(offset, me).wait_send()
        return 0

    lax.fori_loop(1, count, sent, 0)


def scatter_kernel(
    heat_hbm, keys_hbm, wall_ref, coef_ref, cool_ref, out_ref, cool_out,
    heat_sem, keys_ref, keys_sem, edge_ref, edge_sem, start_ref
):
    nx, ny, nz = heat_hbm.shape
    lines, wall = keys_hbm.shape
    keys_load = pltpu.make_async_copy(keys_hbm, keys_ref, keys_sem)
    keys_load.start()
    heat_load = pltpu.make_async_copy(heat_hbm, out_ref, heat_sem)
    heat_load.start()
    plane_shift = log2(lines) + log2(nz) + log2(ny)
    load = pltpu.make_async_copy(keys_hbm, edge_ref, edge_sem)
    load.start()
    share = to_column(0.5 * (1.0 - coef_ref[0:1, 0:lines]))
    cool = to_column(cool_ref[...])
    cool_out[...] = cool_ref[...]

    heat_load.wait()
    load.wait()
    keys_load.wait()
    find_starts(edge_ref, start_ref, plane_shift)

    def visit(b, t):
        line, col, row, plane = fields(keys_ref[pl.ds(b, 1), :], lines, ny, nz)
        mine = iota((lines, wall), 0) == line
        share_row = jnp.sum(jnp.where(mine, share, 0.0), axis=0, keepdims=True)
        cool_row = jnp.sum(jnp.where(mine, cool, 0.0), axis=0, keepdims=True)
        high, low = split(share_row * (cool_row - wall_ref[pl.ds(b, 1), :]))
        at_col = iota((nz, wall), 0) == col
        parts = [
            jnp.where(at_col, part.astype(jnp.float32), 0.0).astype(jnp.bfloat16)
            for part in (high, low)
        ]
        hot = hot_rows(plane, t, row, ny)
        return lax.dot_general(
            jnp.concatenate([hot, hot], axis=1),
            jnp.concatenate(parts, axis=1),
            (((1,), (1,)), ((), ())),
            preferred_element_type=jnp.float32,
        )

    def blocks(group, _):
        places = [group * GROUP + i for i in range(GROUP)]
        planes = [edge_ref[b, 0] >> plane_shift for b in places]
        adds = [visit(b, t) for b, t in zip(places, planes)]
        for t, add in zip(planes, adds):
            out_ref[t] = out_ref[t] + add
        return 0

    lax.fori_loop(0, lines // GROUP, blocks, 0)

    places = [start_ref[t] for t in range(1, nx)]
    adds = [visit(jnp.maximum(b, 0), jnp.where(b < 0, -2, t + 1)) for t, b in enumerate(places)]
    for t, add in enumerate(adds):
        out_ref[t + 1] = out_ref[t + 1] + add


def per_device(count, temp, tags, cond_table, store_table, pos, surf, ratio, flag, entry):
    nx, ny, nz = temp.shape
    f32 = jnp.float32
    lines, wall = pos.shape[1:]
    pos, ratio, flag, entry = pos[0], ratio[None], flag[None], entry[None]
    local = pltpu.CompilerParams(vmem_limit_bytes=LIMIT)
    brick = (nx, ny, nz)
    heated, keys = pl.pallas_call(
        functools.partial(conduct_kernel, count),
        out_shape=(
            jax.ShapeDtypeStruct(brick, f32),
            jax.ShapeDtypeStruct((lines, wall), jnp.int32),
        ),
        in_specs=[HBM, HBM, HBM, HBM, HBM],
        out_specs=(HBM, VMEM),
        scratch_shapes=[
            pltpu.VMEM(brick, f32),
            pltpu.SemaphoreType.DMA((nx,)),
            pltpu.VMEM((lines, wall), jnp.int32),
            pltpu.VMEM(brick, f32),
            pltpu.VMEM(brick, jnp.int32),
            pltpu.SMEM(cond_table.shape, f32),
            pltpu.SMEM(store_table.shape, f32),
            pltpu.VMEM(brick, f32),
            pltpu.VMEM(brick, f32),
            pltpu.VMEM(brick, f32),
            pltpu.VMEM(brick, f32),
            pltpu.VMEM((nx + 1, ny, nz), f32),
            pltpu.VMEM(brick, f32),
            pltpu.VMEM(brick, f32),
            pltpu.VMEM((STEPS, 2, ny, nz), f32),
            pltpu.VMEM((2, ny, nz), jnp.int32),
            pltpu.SemaphoreType.DMA((STEPS + 1, 2, PARTS)),
            pltpu.SemaphoreType.DMA((STEPS + 1, 2, PARTS)),
            pltpu.SemaphoreType.DMA((5,)),
        ],
        compiler_params=pltpu.CompilerParams(
            vmem_limit_bytes=LIMIT, collective_id=0, has_side_effects=True
        ),
        name="conduct",
    )(temp, tags, cond_table, store_table, pos)
    walls, coef = pl.pallas_call(
        gather_kernel,
        out_shape=(
            jax.ShapeDtypeStruct((lines, wall), f32),
            jax.ShapeDtypeStruct((2, 128), f32),
        ),
        in_specs=[HBM, HBM, VMEM, VMEM],
        out_specs=(VMEM, VMEM),
        scratch_shapes=[
            pltpu.VMEM(brick, f32),
            pltpu.SemaphoreType.DMA((nx,)),
            pltpu.VMEM((lines, wall), jnp.int32),
            pltpu.SemaphoreType.DMA,
            pltpu.VMEM((nx, 2 * nz, ny), jnp.bfloat16),
            pltpu.SMEM((lines, wall), jnp.int32),
            pltpu.SemaphoreType.DMA,
            pltpu.SMEM((nx,), jnp.int32),
        ],
        compiler_params=local,
        name="gather",
    )(heated, keys, surf, ratio)
    cool = pl.pallas_call(
        functools.partial(march_kernel, count),
        out_shape=jax.ShapeDtypeStruct((1, lines), f32),
        in_specs=[VMEM, VMEM, VMEM],
        out_specs=VMEM,
        scratch_shapes=[
            pltpu.VMEM((count, 2, 128), f32),
            pltpu.SemaphoreType.DMA((count,)),
            pltpu.SemaphoreType.DMA((count,)),
        ],
        compiler_params=pltpu.CompilerParams(
            vmem_limit_bytes=LIMIT, collective_id=1, has_side_effects=True
        ),
        name="march",
    )(coef, flag, entry)
    final, coolant = pl.pallas_call(
        scatter_kernel,
        out_shape=(
            jax.ShapeDtypeStruct(brick, f32),
            jax.ShapeDtypeStruct((1, lines), f32),
        ),
        in_specs=[HBM, HBM, VMEM, VMEM, VMEM],
        out_specs=(VMEM, VMEM),
        scratch_shapes=[
            pltpu.SemaphoreType.DMA,
            pltpu.VMEM((lines, wall), jnp.int32),
            pltpu.SemaphoreType.DMA,
            pltpu.SMEM((lines, wall), jnp.int32),
            pltpu.SemaphoreType.DMA,
            pltpu.SMEM((nx,), jnp.int32),
        ],
        compiler_params=local,
        name="scatter",
    )(heated, keys, walls, coef, cool)
    return final, coolant


def solution(mesh):
    return jax.shard_map(
        functools.partial(per_device, mesh.shape["brick"]),
        mesh=mesh,
        in_specs=(
            P(("pour", "brick"), None, None),
            P("brick", None, None),
            P(),
            P(),
            P("brick", None, None),
            P("brick", None),
            P(),
            P(),
            P("pour"),
        ),
        out_specs=(P(("pour", "brick"), None, None), P(("pour", "brick"), None)),
        check_vma=False,
    )
```
